1024 devices in a mesh: dp: 16 (over z_hi, y), tensor: 4 (over x), expert: 16 (over z_lo, core).
Axes of the slice: x: 4, y: 4, z: 32 (z_hi: 4, z_lo: 8; z = z_hi * 8 + z_lo), core: 2. Of those that a mesh axis runs over, the one named last changes fastest.
Arguments:
- grad_out: bfloat16 [8192, 4096], P(('tensor', 'expert'), 'dp'), may hold values from -6 to 6
- expert_ids: int32 [8192, 8], P(('tensor', 'expert')), may hold values from 0 to 63, all different within a row; in each aligned block of 128 rows (0 to 127, 128 to 255, ...) at most 24 rows name the same one
- gate_values: float32 [8192, 8], P(('tensor', 'expert')), may hold values from 0.02 to 0.5
- w_down: bfloat16 [64, 4096, 768], P(('tensor', 'expert'), 'dp'), may hold values from -0.09375 to 0.09375
- hidden_slots: bfloat16 [64, 64, 24, 768], P(('tensor', 'expert')), may hold values from -0.29882812 to 0.29882812
Outputs:
- d_hidden: bfloat16 [64, 64, 24, 768], P(('tensor', 'expert'), 'dp')
- d_gate: float32 [8192, 8], P(('tensor', 'expert'))
- d_wdown: bfloat16 [64, 4096, 768], P(('tensor', 'expert'), 'dp')
The draws below stay inside these ranges and needn't reach their ends.
Inputs may be any that keep to these rules, and one draw needn't show every extreme that they name: `expert_ids`: each token names 8 different experts; the tokens of one device name one expert at most 24 times, and some device's tokens name some expert exactly 24 times.
All inputs are finite; a program needn't handle non-finite values.
Results may differ from the reference program's by a relative error of at most 0.02.
Values may be sent and summed in bfloat16 or wider, within the bound.
No kernel may reach another device: no remote copies, remote signals or barrier semaphores. Data moves between devices by JAX's collectives and lax.ppermute only.
A program may use at most 32 MiB of HBM per device.

```python
import math
import jax
import jax.numpy as jnp
import numpy as np
from jax import lax

D = 4096
FF = 768
TOP = 8
TOK_DEV = 128
EXPERTS = 64
CAP = 24
TOKENS = 8192


def steps_of(stream_key, extent, cuts, smallest, top_value):
    loudness, own = 1.0, jax.random.fold_in(stream_key, 6)
    for dim, parts in cuts:
        draws = jnp.exp(jax.random.uniform(jax.random.fold_in(own, dim), (parts,), jnp.float32, smallest / len(cuts), top_value / len(cuts)))
        loudness = loudness * jnp.repeat(draws, extent[dim] // parts).reshape([-1 if axis == dim else 1 for axis in range(len(extent))])
    return loudness


def deal_out(rng, own, number, rows, number_of, top, most, slope):
    order = jax.random.permutation(rng, number_of)
    crowded, usual = shares(number_of, rows * top, most, slope, True), shares(number_of, rows * top, most, slope, False)
    places = jnp.arange(number_of)

    def named(sizes, offset_by):
        used = int((sizes > 0).sum())
        fixed = max(1, used // 4)
        moved = fixed + (places - fixed + offset_by * (used - fixed)) % max(1, number_of - fixed)
        return jnp.zeros((number_of,), jnp.int32).at[order[jnp.where(places < fixed, places, moved)]].set(jnp.asarray(sizes, jnp.int32))

    sizes = jnp.where(number % 4 == 0, named(crowded, number // 4), named(usual, number - number // 4 - 1))
    mixed = jax.random.permutation(jax.random.fold_in(own, 3), number_of)
    donor, sink = mixed[0:number_of // 2 * 2:2], mixed[1:number_of // 2 * 2:2]
    room = jnp.minimum(sizes[donor] - 1, most - sizes[sink]) // 2
    room = jnp.where((donor == order[0]) | (sink == order[0]) | (sizes[sink] == 0), 0, jnp.maximum(room, 0))
    moved = jax.random.randint(jax.random.fold_in(own, 4), (number_of // 2,), 0, 1 << 20) % (room + 1)
    sizes = sizes.at[donor].add(-moved).at[sink].add(moved)
    items = jnp.searchsorted(jnp.cumsum(sizes), jnp.arange(rows * top), side="right").astype(jnp.int32)
    table = items.reshape(top, rows).T
    table = table[jax.random.permutation(jax.random.fold_in(own, 1), rows)]
    offset_by = jax.random.randint(jax.random.fold_in(own, 2), (rows, 1), 0, top)
    return jnp.take_along_axis(table, (jnp.arange(top)[None, :] + offset_by) % top, axis=1)


def shares(number_of, total, bound, skew, full):
    loads = [(1 << 20) // math.isqrt(grade ** skew) + 1 for grade in range(1, number_of + 1)]
    largest = bound if full else min(bound, max(-(-total // number_of), total * loads[0] // sum(loads)))
    least = 1 if total - largest >= number_of - 1 else 0
    given, surplus = [largest] + [least] * (number_of - 1), total - largest - least * (number_of - 1)
    while surplus > 0:
        candidates = [i for i in range(1, number_of) if given[i] < largest] or [i for i in range(1, number_of) if given[i] < bound]
        mass, left = sum([loads[i] for i in candidates]), surplus
        for i in candidates:
            more = min(bound - given[i], max(1, left * loads[i] // mass), surplus)
            given[i] = given[i] + more
            surplus = surplus - more
    return np.array(given)


def normal_values(rng, shape, scale, most, split=(), kind=jnp.bfloat16):
    entries = jax.random.normal(rng, shape, jnp.float32) * scale
    if len(split) > 0:
        entries = steps_of(rng, shape, split, -0.22, 0.18) * entries
    return jnp.clip(entries, min=-most, max=most).astype(kind)


def setup_inputs(seed: int = 0) -> dict:
    streams_of = jax.random.split(jax.random.key(seed), 6)
    grad_out = normal_values(streams_of[0], (TOKENS, D), 1.0, 6.0, ((0, 64), (1, 16)))
    expert_ids_keys = jax.random.split(jax.random.fold_in(streams_of[1], 1), TOKENS // TOK_DEV)
    expert_ids_turns = jax.random.permutation(jax.random.fold_in(streams_of[1], 3), TOKENS // TOK_DEV)
    expert_ids = jax.vmap(lambda own, number: deal_out(jax.random.fold_in(streams_of[1], 2), own, number, TOK_DEV, EXPERTS, TOP, CAP, 2))(expert_ids_keys, expert_ids_turns).reshape((TOKENS, TOP))
    gate_values = jnp.clip(jnp.exp(math.log(0.5) - 3.218876 * jax.random.uniform(streams_of[2], (TOKENS, TOP), jnp.float32) ** steps_of(streams_of[2], (TOKENS, TOP), ((0, 64),), -0.2, 0.2)), 0.02, 0.5)
    w_down = normal_values(streams_of[3], (EXPERTS, D, FF), D ** -0.5, 0.09375, ((0, 64), (1, 16)))
    hidden_slots = normal_values(streams_of[4], (EXPERTS, EXPERTS, CAP, FF), 0.05, 0.29882812, ((0, 64),))
    return {"grad_out": grad_out, "expert_ids": expert_ids, "gate_values": gate_values, "w_down": w_down, "hidden_slots": hidden_slots}


def slot_tables(ids, gates, experts, cap):
    routes = ids.reshape(-1).astype(jnp.int32)
    count = routes.shape[0]
    onehot = (routes[:, None] == jnp.arange(experts, dtype=jnp.int32)[None, :]).astype(jnp.int32)
    before = jnp.cumsum(onehot, axis=0) - onehot
    position = jnp.sum(before * onehot, axis=1).astype(jnp.int32)
    route_slot = routes * cap + position
    match = route_slot[None, :] == jnp.arange(experts * cap, dtype=jnp.int32)[:, None]
    filled = jnp.any(match, axis=1)
    token_of = jnp.arange(count, dtype=jnp.int32) // ids.shape[1]
    owner = jnp.sum(jnp.where(match, token_of[None, :], 0), axis=1).astype(jnp.int32)
    weight = jnp.sum(jnp.where(match, gates.reshape(-1)[None, :], jnp.zeros((), gates.dtype)), axis=1)
    return owner.reshape(experts, cap), filled.reshape(experts, cap), weight.reshape(experts, cap), route_slot


def reference(grad_out, expert_ids, gate_values, w_down, hidden_slots):
    blocks = grad_out.reshape(EXPERTS, TOK_DEV, D)
    ids = expert_ids.reshape(EXPERTS, TOK_DEV, TOP)
    gates = gate_values.reshape(EXPERTS, TOK_DEV, TOP)
    owner, filled, weight, route_slot = jax.vmap(lambda a, b: slot_tables(a, b, EXPERTS, CAP))(ids, gates)
    owner = jnp.swapaxes(owner, 0, 1)
    filled = jnp.swapaxes(filled, 0, 1)
    weight = jnp.swapaxes(weight, 0, 1)
    sources = jnp.arange(EXPERTS, dtype=jnp.int32)[:, None]

    def one_expert(ys):
        own_e, fill_e, wt_e, weights_e, act_e = ys
        rows = blocks[sources, own_e]
        rows = jnp.where(fill_e[:, :, None], rows, jnp.zeros((), rows.dtype)).reshape(-1, D)
        u = jnp.dot(rows, weights_e, preferred_element_type=jnp.float32)
        scale = wt_e.reshape(-1, 1)
        dh = (scale * u).astype(jnp.bfloat16).reshape(EXPERTS, CAP, FF)
        acts = act_e.reshape(-1, FF)
        dg = jnp.sum(acts.astype(jnp.float32) * u, axis=1).reshape(EXPERTS, CAP)
        scaled = (scale * rows.astype(jnp.float32)).astype(jnp.bfloat16)
        grad_w = jnp.dot(scaled.T, acts, preferred_element_type=jnp.float32).astype(jnp.bfloat16)
        return dh, dg, grad_w

    d_hidden, slot_gate, d_wdown = lax.map(one_expert, (owner, filled, weight, w_down, hidden_slots))
    per_source = jnp.swapaxes(slot_gate, 0, 1).reshape(EXPERTS, EXPERTS * CAP)
    d_gate = jnp.take_along_axis(per_source, route_slot, axis=1).reshape(TOKENS, TOP)
    return d_hidden, d_gate, d_wdown
```

```python
import functools

import jax
import jax.numpy as jnp
from jax import lax
from jax.experimental import pallas as pl
from jax.experimental.pallas import tpu as pltpu
from jax.sharding import Mesh
from jax.sharding import PartitionSpec as P

BF16 = jnp.bfloat16
F32 = jnp.float32
EXPERT = ("x", "b2", "b1", "b0", "c")
VMEM_LIMIT = 48 * 1024 * 1024


def call(kernel, outs, in_specs, flops, moved):
    return pl.pallas_call(
        kernel,
        out_shape=outs,
        in_specs=in_specs,
        out_specs=jax.tree.map(lambda _: pl.BlockSpec(memory_space=pltpu.VMEM), outs),
        compiler_params=pltpu.CompilerParams(vmem_limit_bytes=VMEM_LIMIT),
        cost_estimate=pl.CostEstimate(flops=flops, bytes_accessed=moved, transcendentals=0),
    )


def iota(shape, dim):
    return lax.broadcasted_iota(jnp.int32, shape, dim)


def places(ids, experts):
    tokens = ids.shape[1]
    named = jnp.zeros((experts.shape[0], tokens), F32)
    for k in range(ids.shape[0]):
        named = jnp.where(ids[k : k + 1, :] == experts, 1.0, named)
    earlier = (iota((tokens, tokens), 0) < iota((tokens, tokens), 1)).astype(F32)
    before = jnp.dot(named.astype(BF16), earlier.astype(BF16), preferred_element_type=F32)
    return jnp.where(named > 0.0, before.astype(jnp.int32), -1)


def select_kernel(tokens, top, cap, at_ref, *refs):
    blocks, out_ref = refs[:-1], refs[-1]
    near = at_ref[0]
    dests = out_ref.shape[0] // len(blocks)
    d = iota((dests, tokens), 0)
    experts = (d // 4) * 16 + near * 4 + d % 4
    for rel, block in enumerate(blocks):
        below = block[tokens : tokens + 2 * top, :].astype(F32)
        ids = below[:top, :tokens].astype(jnp.int32)
        gates = below[:top, tokens : 2 * tokens] + below[top:, tokens : 2 * tokens]
        place = places(ids, experts)
        weight = jnp.zeros((dests, tokens), F32)
        for k in range(top):
            weight = jnp.where(ids[k : k + 1, :] == experts, gates[k : k + 1, :], weight)
        slot = iota((cap, tokens), 0)
        picks, scales = [], []
        for i in range(dests):
            hit = place[i : i + 1, :] == slot
            picks.append(jnp.where(hit, 1.0, 0.0))
            scales.append(jnp.sum(jnp.where(hit, weight[i : i + 1, :], 0.0), axis=1, keepdims=True))
        picked = jnp.dot(
            jnp.concatenate(picks, axis=0).astype(BF16), block[:tokens, :], preferred_element_type=F32
        )
        index = jnp.bitwise_xor(near, rel)
        for i in range(dests):
            rows = picked[i * cap : (i + 1) * cap, :] * scales[i]
            out_ref[i * len(blocks) + index] = rows.astype(BF16)


def project_kernel(at_ref, rows_ref, w_ref, *outs):
    y, zh = at_ref[1], at_ref[2]
    w = w_ref[...]
    half = w.shape[1] // 2
    groups, share = rows_ref.shape[1], rows_ref.shape[2]
    for k in (2, 1, 3, 0):
        piece = rows_ref[(y + k) % groups].reshape(groups * share, -1)
        u = jnp.dot(piece, w, preferred_element_type=F32).astype(BF16)
        for x in range(groups):
            far = (x + groups - zh) % groups
            outs[2 * k][far] = u[x * share : (x + 1) * share, :half]
            outs[2 * k + 1][far] = u[x * share : (x + 1) * share, half:]


def local_kernel(rows_ref, w_ref, acts_ref, gate_ref, grad_ref):
    groups, share = rows_ref.shape[1], rows_ref.shape[2]
    w = w_ref[...]
    ones = jnp.ones((8, w.shape[1]), F32)
    total = jnp.zeros(w.shape, F32)
    for y in range(groups):
        piece = rows_ref[y].reshape(groups * share, -1)
        acts = acts_ref[:, y].reshape(groups * share, -1)
        u = jnp.dot(piece, w, preferred_element_type=F32)
        product = u * acts.astype(F32)
        line = lax.dot_general(
            ones,
            product,
            (((1,), (1,)), ((), ())),
            precision=lax.Precision.HIGHEST,
            preferred_element_type=F32,
        )
        gate_ref[y : y + 1, :] = line[0:1, :]
        total = total + lax.dot_general(
            piece, acts, (((0,), (0,)), ((), ())), preferred_element_type=F32
        )
    grad_ref[...] = total.astype(BF16)


def route_kernel(ids_ref, gates_ref, returned_ref, out_ref):
    ids, gates = ids_ref[...], gates_ref[...]
    experts, cap = returned_ref.shape
    tokens = ids.shape[1]
    e = iota((experts, tokens), 0)
    place = places(ids, e)
    returned = returned_ref[...]
    found = jnp.zeros((experts, tokens), F32)
    for p in range(cap):
        found = jnp.where(place == p, returned[:, p : p + 1], found)
    for k in range(ids.shape[0]):
        mine = jnp.where(ids[k : k + 1, :] == e, found, 0.0)
        out_ref[k : k + 1, :] = jnp.sum(mine, axis=0, keepdims=True) / gates[k : k + 1, :]


def swap(value, axis, bit=1):
    return lax.ppermute(value, axis, [(i, i ^ bit) for i in range(lax.axis_size(axis))])


def shift(value, axis, by):
    size = lax.axis_size(axis)
    return lax.ppermute(value, axis, [(i, (i + by) % size) for i in range(size)])


def add(*parts):
    return functools.reduce(jnp.add, [p.astype(F32) for p in parts])


def ring_sum(a, b, axis):
    a2 = shift(a[2], axis, 1)
    b2 = shift(b[2], axis, -1)
    b1 = shift(b[1], axis, 1)
    a3 = shift(a[3], axis, -1)
    a1 = shift(add(a[1], a2).astype(BF16), axis, 1)
    b3 = shift(add(b[3], b2).astype(BF16), axis, -1)
    return add(a[0], a1, a3), add(b[0], b3, b1)


def on_device(grad_out, expert_ids, gate_values, w_down, hidden_slots):
    tokens, width = grad_out.shape
    top = expert_ids.shape[1]
    _, sources, cap, hidden = hidden_slots.shape
    near = lax.axis_index("b2") * 2 + lax.axis_index("b1")
    at = jnp.stack([near, lax.axis_index("y"), lax.axis_index("zh")]).astype(jnp.int32)
    smem = pl.BlockSpec(memory_space=pltpu.SMEM)
    vmem = pl.BlockSpec(memory_space=pltpu.VMEM)

    ids = expert_ids.T
    gates = gate_values.T
    high = gates.astype(BF16)
    low = (gates - high.astype(F32)).astype(BF16)
    below = jnp.concatenate([ids.astype(BF16), ids.astype(BF16)], axis=0)
    block = jnp.concatenate(
        [grad_out, jnp.concatenate([below, jnp.concatenate([high, low], axis=0)], axis=1)], axis=0
    )
    over_b1 = swap(block, "b1")
    over_b2 = swap(block, "b2")
    over_both = swap(over_b2, "b1")

    picked = call(
        functools.partial(select_kernel, tokens, top, cap),
        jax.ShapeDtypeStruct((sources, cap, width), BF16),
        [smem] + [vmem] * 4,
        2 * sources * cap * tokens * width,
        3 * sources * cap * width,
    )(at, block, over_b1, over_b2, over_both)
    rows = lax.all_to_all(
        picked.reshape(16, 4, cap, width), ("x", "b0", "c"), split_axis=0, concat_axis=0, tiled=True
    )
    rows = rows.reshape(4, 4, 4, cap, width).transpose(2, 0, 1, 3, 4).reshape(4, 4, 4 * cap, width)

    w = w_down[0]
    pieces = call(
        project_kernel,
        [jax.ShapeDtypeStruct((4, 4 * cap, hidden // 2), BF16)] * 8,
        [smem, vmem, vmem],
        2 * sources * cap * width * hidden,
        2 * sources * cap * (width + hidden),
    )(at, rows, w)
    gate_part, d_wdown = call(
        local_kernel,
        [jax.ShapeDtypeStruct((4, 16 * cap), F32), jax.ShapeDtypeStruct((width, hidden), BF16)],
        [vmem] * 3,
        4 * sources * cap * width * hidden,
        2 * sources * cap * (width + hidden),
    )(rows, w, hidden_slots.reshape(4, 4, 4 * cap, hidden))

    a, b = ring_sum(pieces[0::2], pieces[1::2], "y")
    a, b = a.astype(BF16), b.astype(BF16)
    a, b = ring_sum(a, b, "zh")
    d_hidden = jnp.concatenate([a, b], axis=1).astype(BF16).reshape(1, 4, cap, hidden)

    gate_part = gate_part.reshape(4, 4, 4 * cap).transpose(1, 0, 2).reshape(sources, cap)
    returned = lax.all_to_all(gate_part, EXPERT, split_axis=0, concat_axis=0, tiled=True)
    d_gate = call(
        route_kernel,
        jax.ShapeDtypeStruct((top, tokens), F32),
        [vmem] * 3,
        1 << 20,
        1 << 16,
    )(ids, gates, returned)
    for axis in ("y", "zh"):
        for bit in (1, 2):
            d_gate = d_gate + swap(d_gate, axis, bit)
    return d_hidden, d_gate.T, d_wdown[None]


def solution(mesh):
    fine = Mesh(mesh.devices.reshape(4, 4, 4, 2, 2, 2, 2), ("zh", "y") + EXPERT)
    dp = ("zh", "y")
    return jax.shard_map(
        on_device,
        mesh=fine,
        in_specs=(
            P(EXPERT, dp),
            P(EXPERT, None),
            P(EXPERT, None),
            P(EXPERT, dp, None),
            P(EXPERT, None, None, None),
        ),
        out_specs=(P(EXPERT, dp, None, None), P(EXPERT, None), P(EXPERT, dp, None)),
        check_vma=False,
    )
```

```python
import functools

import jax
import jax.numpy as jnp
from jax import lax
from jax.experimental import pallas as pl
from jax.experimental.pallas import tpu as pltpu
from jax.sharding import Mesh
from jax.sharding import PartitionSpec as P

BF16 = jnp.bfloat16
F32 = jnp.float32
EXPERT = ("x", "b2", "b1", "b0", "c")
VMEM_LIMIT = 48 * 1024 * 1024


def call(kernel, outs, in_specs, flops, moved):
    return pl.pallas_call(
        kernel,
        out_shape=outs,
        in_specs=in_specs,
        out_specs=jax.tree.map(lambda _: pl.BlockSpec(memory_space=pltpu.VMEM), outs),
        compiler_params=pltpu.CompilerParams(vmem_limit_bytes=VMEM_LIMIT),
        cost_estimate=pl.CostEstimate(flops=flops, bytes_accessed=moved, transcendentals=0),
    )


def iota(shape, dim):
    return lax.broadcasted_iota(jnp.int32, shape, dim)


def places(ids, experts):
    tokens = ids.shape[1]
    named = jnp.zeros((experts.shape[0], tokens), F32)
    for k in range(ids.shape[0]):
        named = jnp.where(ids[k : k + 1, :] == experts, 1.0, named)
    earlier = (iota((tokens, tokens), 0) < iota((tokens, tokens), 1)).astype(F32)
    before = jnp.dot(named.astype(BF16), earlier.astype(BF16), preferred_element_type=F32)
    return jnp.where(named > 0.0, before.astype(jnp.int32), -1)


def group(near, shape):
    d = iota(shape, 0)
    return (d // 4) * 16 + near * 4 + d % 4


def pack_kernel(grad_ref, ids_ref, gates_ref, out_ref):
    tokens = grad_ref.shape[0]
    ids = ids_ref[...].astype(F32)
    gates = gates_ref[...]
    high = gates.astype(BF16).astype(F32)
    out_ref[:tokens, :] = grad_ref[...]
    left = jnp.concatenate([ids, ids], axis=0)
    right = jnp.concatenate([high, gates - high], axis=0)
    out_ref[tokens:, :] = jnp.concatenate([left, right], axis=1).astype(BF16)


def select_kernel(tokens, top, cap, at_ref, *refs):
    blocks, out_ref = refs[:-1], refs[-1]
    near = at_ref[0]
    dests = out_ref.shape[0] // len(blocks)
    experts = group(near, (dests, tokens))
    below = blocks[0][tokens : tokens + 2 * top, :].astype(F32)
    ids = below[:top, :tokens].astype(jnp.int32)
    gates = below[:top, tokens : 2 * tokens] + below[top:, tokens : 2 * tokens]
    place = places(ids, experts)
    weight = jnp.zeros((dests, tokens), F32)
    for k in range(top):
        weight = jnp.where(ids[k : k + 1, :] == experts, gates[k : k + 1, :], weight)
    slot = iota((cap, tokens), 0)
    picks, scales = [], []
    for i in range(dests):
        hit = place[i : i + 1, :] == slot
        picks.append(jnp.where(hit, 1.0, 0.0))
        scales.append(jnp.sum(jnp.where(hit, weight[i : i + 1, :], 0.0), axis=1, keepdims=True))
    picks = jnp.concatenate(picks, axis=0).astype(BF16)
    for rel, block in enumerate(blocks):
        picked = jnp.dot(picks, block[:tokens, :], preferred_element_type=F32)
        index = jnp.bitwise_xor(near, rel)
        for i in range(dests):
            rows = picked[i * cap : (i + 1) * cap, :] * scales[i]
            out_ref[i * len(blocks) + index] = rows.astype(BF16)


def project_kernel(at_ref, rows_ref, *refs):
    ws, outs = refs[:4], refs[4:]
    y, zh = at_ref[1], at_ref[2]
    u = jnp.zeros((rows_ref.shape[1], ws[0].shape[1]), F32)
    for k in range(4):
        u = u + jnp.dot(rows_ref[(y + 4 - k) % 4], ws[k][...], preferred_element_type=F32)
    u = u.astype(BF16)
    share, half = u.shape[0] // 4, u.shape[1] // 2
    for x in range(4):
        far = (x + 4 - zh) % 4
        for side in range(2):
            outs[side][far] = u[x * share : (x + 1) * share, side * half : (side + 1) * half]


def gate_kernel(at_ref, a_ref, b_ref, acts_ref, gate_ref):
    y, zh = at_ref[1], at_ref[2]
    half = a_ref.shape[2]
    ones = jnp.ones((8, half), F32)
    for x in range(4):
        far = (x + 4 - zh) % 4
        acts = acts_ref[x, y].astype(F32)
        product = a_ref[far].astype(F32) * acts[:, :half] + b_ref[far].astype(F32) * acts[:, half:]
        line = lax.dot_general(
            ones,
            product,
            (((1,), (1,)), ((), ())),
            precision=lax.Precision.HIGHEST,
            preferred_element_type=F32,
        )
        gate_ref[x : x + 1, :] = line[0:1, :]


def weights_kernel(at_ref, rows_ref, acts_ref, *outs):
    y = at_ref[1]
    acts = acts_ref[:, y].reshape(rows_ref.shape[1], -1)
    for k in range(4):
        part = lax.dot_general(
            rows_ref[(y + k) % 4], acts, (((0,), (0,)), ((), ())), preferred_element_type=F32
        )
        outs[k][...] = part.astype(BF16)


def route_kernel(at_ref, ids_ref, gates_ref, *refs):
    parts, out_ref = refs[:-1], refs[-1]
    y = at_ref[1]
    ids, gates = ids_ref[...], gates_ref[...]
    shape = (parts[0].shape[0], ids.shape[1])
    lines = [jnp.zeros((1, shape[1]), F32)] * ids.shape[0]
    for rel, part in enumerate(parts):
        experts = group(jnp.bitwise_xor(y, rel), shape)
        place = places(ids, experts)
        values = part[...]
        found = jnp.zeros(shape, F32)
        for p in range(values.shape[1]):
            found = jnp.where(place == p, values[:, p : p + 1], found)
        for k in range(ids.shape[0]):
            mine = jnp.where(ids[k : k + 1, :] == experts, found, 0.0)
            lines[k] = lines[k] + jnp.sum(mine, axis=0, keepdims=True)
    for k in range(ids.shape[0]):
        out_ref[k : k + 1, :] = lines[k] / gates[k : k + 1, :]


def across(value, back, rel):
    pairs = [(y * 4 + beta, beta * 4 + (y ^ rel)) for y in range(4) for beta in range(4)]
    if back:
        pairs = [(there, here) for here, there in pairs]
    return lax.ppermute(value, ("y", "b2", "b1"), pairs)


def shift(value, axis, by):
    size = lax.axis_size(axis)
    return lax.ppermute(value, axis, [(i, (i + by) % size) for i in range(size)])


def add(*parts):
    return functools.reduce(jnp.add, [p.astype(F32) for p in parts])


def ring_sum(a, b, axis):
    a2 = shift(a[2], axis, 1)
    b2 = shift(b[2], axis, -1)
    b1 = shift(b[1], axis, 1)
    a3 = shift(a[3], axis, -1)
    a1 = shift(add(a[1], a2).astype(BF16), axis, 1)
    b3 = shift(add(b[3], b2).astype(BF16), axis, -1)
    return add(a[0], a1, a3), add(b[0], b3, b1)


def on_device(grad_out, expert_ids, gate_values, w_down, hidden_slots):
    tokens, width = grad_out.shape
    top = expert_ids.shape[1]
    _, sources, cap, hidden = hidden_slots.shape
    near = lax.axis_index("b2") * 2 + lax.axis_index("b1")
    at = jnp.stack([near, lax.axis_index("y"), lax.axis_index("zh")]).astype(jnp.int32)
    smem = pl.BlockSpec(memory_space=pltpu.SMEM)
    vmem = pl.BlockSpec(memory_space=pltpu.VMEM)
    ids, gates = expert_ids.T, gate_values.T
    group_of = ("x", "b0", "c")
    slots = sources // 4 * cap

    block = call(
        pack_kernel,
        jax.ShapeDtypeStruct((tokens + 2 * top, width), BF16),
        [vmem] * 3,
        0,
        1 << 18,
    )(grad_out, ids, gates)
    blocks = [across(block, False, rel) for rel in range(4)]
    w = w_down[0]
    ws = [w] + [shift(w, "y", k) for k in (1, 2, 3)]

    picked = call(
        functools.partial(select_kernel, tokens, top, cap),
        jax.ShapeDtypeStruct((sources, cap, width), BF16),
        [smem] + [vmem] * 4,
        2 * sources * cap * tokens * width,
        3 * sources * cap * width,
    )(at, *blocks)
    rows = lax.all_to_all(
        picked.reshape(16, 4, cap, width), group_of, split_axis=0, concat_axis=0, tiled=True
    )
    rows = rows.transpose(1, 0, 2, 3).reshape(4, slots, width)

    a, b = call(
        project_kernel,
        [jax.ShapeDtypeStruct((4, slots // 4, hidden // 2), BF16)] * 2,
        [smem] + [vmem] * 5,
        8 * slots * width * hidden,
        8 * slots * width,
    )(at, rows, *ws)
    acts = hidden_slots.reshape(4, 4, slots // 4, hidden)
    gate_part = call(
        gate_kernel,
        jax.ShapeDtypeStruct((4, slots // 4), F32),
        [smem] + [vmem] * 3,
        2 * slots * hidden,
        4 * slots * hidden,
    )(at, a, b, acts)
    a, b = ring_sum(a, b, "zh")
    d_hidden = jnp.concatenate([a, b], axis=1).astype(BF16).reshape(1, 4, cap, hidden)

    returned = lax.all_to_all(
        gate_part.reshape(16, cap), group_of, split_axis=0, concat_axis=0, tiled=True
    )
    d_gate = call(
        route_kernel,
        jax.ShapeDtypeStruct((top, tokens), F32),
        [smem] + [vmem] * 6,
        1 << 20,
        1 << 16,
    )(at, ids, gates, *[across(returned, True, rel) for rel in range(4)])
    d_gate = add(d_gate, *[shift(d_gate, "zh", k) for k in (1, 2, 3)])

    parts = call(
        weights_kernel,
        [jax.ShapeDtypeStruct((width, hidden), BF16)] * 4,
        [smem] + [vmem] * 2,
        8 * slots * width * hidden,
        8 * slots * width,
    )(at, rows, acts)
    d_wdown = add(parts[0], *[shift(parts[k], "y", k) for k in (1, 2, 3)]).astype(BF16)
    return d_hidden, d_gate.T, d_wdown[None]


def solution(mesh):
    fine = Mesh(mesh.devices.reshape(4, 4, 4, 2, 2, 2, 2), ("zh", "y") + EXPERT)
    dp = ("zh", "y")
    return jax.shard_map(
        on_device,
        mesh=fine,
        in_specs=(
            P(EXPERT, dp),
            P(EXPERT, None),
            P(EXPERT, None),
            P(EXPERT, dp, None),
            P(EXPERT, None, None, None),
        ),
        out_specs=(P(EXPERT, dp, None, None), P(EXPERT, None), P(EXPERT, dp, None)),
        check_vma=False,
    )
```

```python
import functools

import jax
import jax.numpy as jnp
from jax import lax
from jax.experimental import pallas as pl
from jax.experimental.pallas import tpu as pltpu
from jax.sharding import Mesh
from jax.sharding import PartitionSpec as P

BF16 = jnp.bfloat16
F32 = jnp.float32
EXPERT = ("x", "b2", "b1", "b0", "c")
VMEM_LIMIT = 16 * 1024 * 1024


def call(kernel, outs, in_specs, flops, moved):
    return pl.pallas_call(
        kernel,
        out_shape=outs,
        in_specs=in_specs,
        out_specs=jax.tree.map(lambda _: pl.BlockSpec(memory_space=pltpu.VMEM), outs),
        compiler_params=pltpu.CompilerParams(vmem_limit_bytes=VMEM_LIMIT),
        cost_estimate=pl.CostEstimate(flops=flops, bytes_accessed=moved, transcendentals=0),
    )


def iota(shape, dim):
    return lax.broadcasted_iota(jnp.int32, shape, dim)


def places(ids, experts):
    tokens = ids.shape[1]
    named = jnp.zeros((experts.shape[0], tokens), F32)
    for k in range(ids.shape[0]):
        named = jnp.where(ids[k : k + 1, :] == experts, 1.0, named)
    earlier = (iota((tokens, tokens), 0) < iota((tokens, tokens), 1)).astype(F32)
    before = jnp.dot(named.astype(BF16), earlier.astype(BF16), preferred_element_type=F32)
    return jnp.where(named > 0.0, before.astype(jnp.int32), -1)


def group(near, shape):
    d = iota(shape, 0)
    return (d // 4) * 16 + near * 4 + d % 4


def pack_kernel(grad_ref, ids_ref, gates_ref, out_ref):
    tokens = grad_ref.shape[0]
    ids = ids_ref[...].astype(F32)
    gates = gates_ref[...]
    high = gates.astype(BF16).astype(F32)
    out_ref[:tokens, :] = grad_ref[...]
    left = jnp.concatenate([ids, ids], axis=0)
    right = jnp.concatenate([high, gates - high], axis=0)
    out_ref[tokens:, :] = jnp.concatenate([left, right], axis=1).astype(BF16)


def select_kernel(tokens, top, cap, at_ref, *refs):
    blocks, out_ref = refs[:-1], refs[-1]
    near = at_ref[0]
    dests, width = out_ref.shape[0], blocks[0].shape[1]
    experts = group(near, (dests, tokens))
    below = blocks[0][tokens : tokens + 2 * top, :].astype(F32)
    ids = below[:top, :tokens].astype(jnp.int32)
    gates = below[:top, tokens : 2 * tokens] + below[top:, tokens : 2 * tokens]
    place = places(ids, experts)
    weight = jnp.zeros((dests, tokens), F32)
    for k in range(top):
        weight = jnp.where(ids[k : k + 1, :] == experts, gates[k : k + 1, :], weight)
    slot = iota((cap, tokens), 0)
    picks, scales = [], []
    for i in range(dests):
        hit = place[i : i + 1, :] == slot
        picks.append(jnp.where(hit, 1.0, 0.0))
        scales.append(jnp.sum(jnp.where(hit, weight[i : i + 1, :], 0.0), axis=1, keepdims=True))
    picks = jnp.concatenate(picks, axis=0).astype(BF16)
    for rel, block in enumerate(blocks):
        picked = jnp.dot(picks, block[:tokens, :], preferred_element_type=F32)
        lanes = pl.ds(pl.multiple_of(jnp.bitwise_xor(near, rel) * width, width), width)
        for i in range(dests):
            rows = picked[i * cap : (i + 1) * cap, :] * scales[i]
            out_ref[i, :, lanes] = rows.astype(BF16)


def project_kernel(at_ref, rows_ref, *refs):
    ws, outs = refs[:4], refs[4:]
    y, zh = at_ref[1], at_ref[2]
    width = ws[0].shape[0]
    u = jnp.zeros((rows_ref.shape[0], ws[0].shape[1]), F32)
    for k in range(4):
        lanes = pl.ds(pl.multiple_of((y + 4 - k) % 4 * width, width), width)
        u = u + jnp.dot(rows_ref[:, lanes], ws[k][...], preferred_element_type=F32)
    u = u.astype(BF16)
    share, half = u.shape[0] // 4, u.shape[1] // 2
    for x in range(4):
        far = (x + 4 - zh) % 4
        for side in range(2):
            outs[side][far] = u[x * share : (x + 1) * share, side * half : (side + 1) * half]


def gate_kernel(at_ref, a_ref, b_ref, acts_ref, gate_ref):
    y, zh = at_ref[1], at_ref[2]
    half = a_ref.shape[2]
    ones = jnp.ones((8, half), F32)
    for x in range(4):
        far = (x + 4 - zh) % 4
        acts = acts_ref[x, y].astype(F32)
        product = a_ref[far].astype(F32) * acts[:, :half] + b_ref[far].astype(F32) * acts[:, half:]
        line = lax.dot_general(
            ones,
            product,
            (((1,), (1,)), ((), ())),
            precision=lax.Precision.HIGHEST,
            preferred_element_type=F32,
        )
        gate_ref[x : x + 1, :] = line[0:1, :]


def weights_kernel(at_ref, rows_ref, acts_ref, *outs):
    y = at_ref[1]
    acts = acts_ref[:, y].reshape(rows_ref.shape[0], -1)
    width = outs[0].shape[0]
    for k in range(4):
        lanes = pl.ds(pl.multiple_of((y + k) % 4 * width, width), width)
        part = lax.dot_general(
            rows_ref[:, lanes], acts, (((0,), (0,)), ((), ())), preferred_element_type=F32
        )
        outs[k][...] = part.astype(BF16)


def route_kernel(at_ref, ids_ref, gates_ref, *refs):
    parts, out_ref = refs[:-1], refs[-1]
    y = at_ref[1]
    ids, gates = ids_ref[...], gates_ref[...]
    shape = (parts[0].shape[0], ids.shape[1])
    lines = [jnp.zeros((1, shape[1]), F32)] * ids.shape[0]
    for rel, part in enumerate(parts):
        experts = group(jnp.bitwise_xor(y, rel), shape)
        place = places(ids, experts)
        values = part[...]
        found = jnp.zeros(shape, F32)
        for p in range(values.shape[1]):
            found = jnp.where(place == p, values[:, p : p + 1], found)
        for k in range(ids.shape[0]):
            mine = jnp.where(ids[k : k + 1, :] == experts, found, 0.0)
            lines[k] = lines[k] + jnp.sum(mine, axis=0, keepdims=True)
    for k in range(ids.shape[0]):
        out_ref[k : k + 1, :] = lines[k] / gates[k : k + 1, :]


def across(value, back, rel):
    pairs = [(y * 4 + beta, beta * 4 + (y ^ rel)) for y in range(4) for beta in range(4)]
    if back:
        pairs = [(there, here) for here, there in pairs]
    return lax.ppermute(value, ("y", "b2", "b1"), pairs)


def shift(value, axis, by):
    size = lax.axis_size(axis)
    return lax.ppermute(value, axis, [(i, (i + by) % size) for i in range(size)])


def add(*parts):
    return functools.reduce(jnp.add, [p.astype(F32) for p in parts])


def on_device(grad_out, expert_ids, gate_values, w_down, hidden_slots):
    tokens, width = grad_out.shape
    top = expert_ids.shape[1]
    _, sources, cap, hidden = hidden_slots.shape
    near = lax.axis_index("b2") * 2 + lax.axis_index("b1")
    at = jnp.stack([near, lax.axis_index("y"), lax.axis_index("zh")]).astype(jnp.int32)
    smem = pl.BlockSpec(memory_space=pltpu.SMEM)
    vmem = pl.BlockSpec(memory_space=pltpu.VMEM)
    ids, gates = expert_ids.T, gate_values.T
    group_of = ("x", "b0", "c")
    slots = sources // 4 * cap

    block = call(
        pack_kernel,
        jax.ShapeDtypeStruct((tokens + 2 * top, width), BF16),
        [pl.BlockSpec()] * 3,
        0,
        1 << 18,
    )(grad_out, ids, gates)
    w = w_down[0]
    blocks = [across(block, False, rel) for rel in range(4)]
    below = shift(w, "y", 1)
    blocks, below = lax.optimization_barrier((blocks, below))

    picked = call(
        functools.partial(select_kernel, tokens, top, cap),
        jax.ShapeDtypeStruct((16, cap, 4 * width), BF16),
        [smem] + [vmem] * 4,
        2 * sources * cap * tokens * width,
        3 * sources * cap * width,
    )(at, *blocks)
    rows = lax.all_to_all(picked, group_of, split_axis=0, concat_axis=0, tiled=True)
    rows = rows.reshape(slots, 4 * width)
    ws = [w, below, shift(w, "y", 2), shift(w, "y", -1)]

    a, b = call(
        project_kernel,
        [jax.ShapeDtypeStruct((4, slots // 4, hidden // 2), BF16)] * 2,
        [smem] + [vmem] * 5,
        8 * slots * width * hidden,
        8 * slots * width,
    )(at, rows, *ws)
    acts = hidden_slots.reshape(4, 4, slots // 4, hidden)
    gate_part = call(
        gate_kernel,
        jax.ShapeDtypeStruct((4, slots // 4), F32),
        [smem] + [vmem] * 3,
        2 * slots * hidden,
        4 * slots * hidden,
    )(at, a, b, acts)
    parts = call(
        weights_kernel,
        [jax.ShapeDtypeStruct((width, hidden), BF16)] * 4,
        [smem] + [vmem] * 2,
        8 * slots * width * hidden,
        8 * slots * width,
    )(at, rows, acts)

    a2, b2, part2 = shift(a[2], "zh", 1), shift(b[2], "zh", -1), shift(parts[2], "y", 2)
    returned = lax.all_to_all(
        gate_part.reshape(16, cap), group_of, split_axis=0, concat_axis=0, tiled=True
    )
    a, b, parts, a2, b2, part2, returned = lax.optimization_barrier(
        (a, b, parts, a2, b2, part2, returned)
    )
    b1, a3, part1 = shift(b[1], "zh", 1), shift(a[3], "zh", -1), shift(parts[1], "y", 1)
    found = [across(returned, True, rel) for rel in range(4)]
    a1, b3 = add(a[1], a2).astype(BF16), add(b[3], b2).astype(BF16)
    a1, b3, parts, b1, a3, part1, found = lax.optimization_barrier(
        (a1, b3, parts, b1, a3, part1, found)
    )
    a1, b3, part3 = shift(a1, "zh", 1), shift(b3, "zh", -1), shift(parts[3], "y", -1)
    d_gate = call(
        route_kernel,
        jax.ShapeDtypeStruct((top, tokens), F32),
        [smem] + [vmem] * 6,
        1 << 20,
        1 << 16,
    )(at, ids, gates, *found)
    d_gate = add(d_gate, *[shift(d_gate, "zh", k) for k in (1, 2, 3)])
    d_hidden = jnp.concatenate([add(a[0], a1, a3), add(b[0], b3, b1)], axis=1)
    d_hidden = d_hidden.astype(BF16).reshape(1, 4, cap, hidden)
    d_wdown = add(parts[0], part1, part2, part3).astype(BF16)
    return d_hidden, d_gate.T, d_wdown[None]


def solution(mesh):
    fine = Mesh(mesh.devices.reshape(4, 4, 4, 2, 2, 2, 2), ("zh", "y") + EXPERT)
    dp = ("zh", "y")
    return jax.shard_map(
        on_device,
        mesh=fine,
        in_specs=(
            P(EXPERT, dp),
            P(EXPERT, None),
            P(EXPERT, None),
            P(EXPERT, dp, None),
            P(EXPERT, None, None, None),
        ),
        out_specs=(P(EXPERT, dp, None, None), P(EXPERT, None), P(EXPERT, dp, None)),
        check_vma=False,
    )
```

```python
import functools

import jax
import jax.numpy as jnp
from jax import lax
from jax.experimental import pallas as pl
from jax.experimental.pallas import tpu as pltpu
from jax.sharding import Mesh
from jax.sharding import PartitionSpec as P

BF16 = jnp.bfloat16
F32 = jnp.float32
EXPERT = ("x", "b2", "b1", "b0", "c")
VMEM_LIMIT = 16 * 1024 * 1024


def call(kernel, outs, in_specs, flops, moved):
    return pl.pallas_call(
        kernel,
        out_shape=outs,
        in_specs=in_specs,
        out_specs=jax.tree.map(lambda _: pl.BlockSpec(memory_space=pltpu.VMEM), outs),
        compiler_params=pltpu.CompilerParams(vmem_limit_bytes=VMEM_LIMIT),
        cost_estimate=pl.CostEstimate(flops=flops, bytes_accessed=moved, transcendentals=0),
    )


def iota(shape, dim):
    return lax.broadcasted_iota(jnp.int32, shape, dim)


def places(ids, experts):
    tokens = ids.shape[1]
    named = jnp.zeros((experts.shape[0], tokens), F32)
    for k in range(ids.shape[0]):
        named = jnp.where(ids[k : k + 1, :] == experts, 1.0, named)
    earlier = (iota((tokens, tokens), 0) < iota((tokens, tokens), 1)).astype(F32)
    before = jnp.dot(named.astype(BF16), earlier.astype(BF16), preferred_element_type=F32)
    return jnp.where(named > 0.0, before.astype(jnp.int32), -1)


def group(near, shape):
    d = iota(shape, 0)
    return (d // 4) * 16 + near * 4 + d % 4


def pack_kernel(grad_ref, ids_ref, gates_ref, out_ref):
    tokens = grad_ref.shape[0]
    ids = ids_ref[...].astype(F32)
    gates = gates_ref[...]
    high = gates.astype(BF16).astype(F32)
    out_ref[:tokens, :] = grad_ref[...]
    left = jnp.concatenate([ids, ids], axis=0)
    right = jnp.concatenate([high, gates - high], axis=0)
    out_ref[tokens:, :] = jnp.concatenate([left, right], axis=1).astype(BF16)


def select_kernel(tokens, top, cap, at_ref, *refs):
    blocks, out_ref = refs[:-1], refs[-1]
    near = at_ref[0]
    dests, width = out_ref.shape[0], blocks[0].shape[1]
    experts = group(near, (dests, tokens))
    below = blocks[0][tokens : tokens + 2 * top, :].astype(F32)
    ids = below[:top, :tokens].astype(jnp.int32)
    gates = below[:top, tokens : 2 * tokens] + below[top:, tokens : 2 * tokens]
    place = places(ids, experts)
    weight = jnp.zeros((dests, tokens), F32)
    for k in range(top):
        weight = jnp.where(ids[k : k + 1, :] == experts, gates[k : k + 1, :], weight)
    slot = iota((cap, tokens), 0)
    picks, scales = [], []
    for i in range(dests):
        hit = place[i : i + 1, :] == slot
        picks.append(jnp.where(hit, 1.0, 0.0))
        scales.append(jnp.sum(jnp.where(hit, weight[i : i + 1, :], 0.0), axis=1, keepdims=True))
    picks = jnp.concatenate(picks, axis=0).astype(BF16)
    for rel, block in enumerate(blocks):
        picked = jnp.dot(picks, block[:tokens, :], preferred_element_type=F32)
        lanes = pl.ds(pl.multiple_of(jnp.bitwise_xor(near, rel) * width, width), width)
        for i in range(dests):
            rows = picked[i * cap : (i + 1) * cap, :] * scales[i]
            out_ref[i, :, lanes] = rows.astype(BF16)


def project_kernel(at_ref, rows_ref, w_ref, *outs):
    zh = at_ref[2]
    u = jnp.dot(rows_ref[...], w_ref[...], preferred_element_type=F32).astype(BF16)
    share, half = u.shape[0] // 4, u.shape[1] // 2
    for x in range(4):
        far = (x + 4 - zh) % 4
        for side in range(2):
            outs[side][far] = u[x * share : (x + 1) * share, side * half : (side + 1) * half]


def gate_kernel(at_ref, a_ref, b_ref, acts_ref, gate_ref):
    y, zh = at_ref[1], at_ref[2]
    half = a_ref.shape[2]
    ones = jnp.ones((8, half), F32)
    for x in range(4):
        far = (x + 4 - zh) % 4
        acts = acts_ref[x, y].astype(F32)
        product = a_ref[far].astype(F32) * acts[:, :half] + b_ref[far].astype(F32) * acts[:, half:]
        line = lax.dot_general(
            ones,
            product,
            (((1,), (1,)), ((), ())),
            precision=lax.Precision.HIGHEST,
            preferred_element_type=F32,
        )
        gate_ref[x : x + 1, :] = line[0:1, :]


def weights_kernel(at_ref, rows_ref, acts_ref, out_ref):
    acts = acts_ref[:, at_ref[1]].reshape(rows_ref.shape[0], -1)
    part = lax.dot_general(
        rows_ref[...], acts, (((0,), (0,)), ((), ())), preferred_element_type=F32
    )
    out_ref[...] = part.astype(BF16)


def route_kernel(at_ref, ids_ref, gates_ref, *refs):
    parts, out_ref, rider_ref = refs[:-2], refs[-2], refs[-1]
    y = at_ref[1]
    ids, gates = ids_ref[...], gates_ref[...]
    shape = (parts[0].shape[0], ids.shape[1])
    lines = [jnp.zeros((1, shape[1]), F32)] * ids.shape[0]
    for rel, part in enumerate(parts):
        experts = group(jnp.bitwise_xor(y, rel), shape)
        place = places(ids, experts)
        values = part[...]
        found = jnp.zeros(shape, F32)
        for p in range(values.shape[1]):
            found = jnp.where(place == p, values[:, p : p + 1], found)
        for k in range(ids.shape[0]):
            mine = jnp.where(ids[k : k + 1, :] == experts, found, 0.0)
            lines[k] = lines[k] + jnp.sum(mine, axis=0, keepdims=True)
    part = jnp.concatenate(lines, axis=0) / gates
    high = part.astype(BF16).astype(F32)
    out_ref[...] = part
    rider = jnp.concatenate([high, part - high, jnp.zeros_like(part)], axis=1)
    rider_ref[...] = jnp.concatenate([rider, jnp.zeros_like(rider)], axis=0).astype(BF16)


def across(value, back, rel):
    pairs = [(y * 4 + beta, beta * 4 + (y ^ rel)) for y in range(4) for beta in range(4)]
    if back:
        pairs = [(there, here) for here, there in pairs]
    return lax.ppermute(value, ("y", "b2", "b1"), pairs)


def shift(value, axis, by):
    size = lax.axis_size(axis)
    return lax.ppermute(value, axis, [(i, (i + by) % size) for i in range(size)])


def add(*parts):
    return functools.reduce(jnp.add, [p.astype(F32) for p in parts])


def on_device(grad_out, expert_ids, gate_values, w_down, hidden_slots):
    tokens, width = grad_out.shape
    top = expert_ids.shape[1]
    _, sources, cap, hidden = hidden_slots.shape
    near = lax.axis_index("b2") * 2 + lax.axis_index("b1")
    at = jnp.stack([near, lax.axis_index("y"), lax.axis_index("zh")]).astype(jnp.int32)
    smem = pl.BlockSpec(memory_space=pltpu.SMEM)
    vmem = pl.BlockSpec(memory_space=pltpu.VMEM)
    ids, gates = expert_ids.T, gate_values.T
    group_of = ("x", "b0", "c")
    slots = sources // 4 * cap

    block = call(
        pack_kernel,
        jax.ShapeDtypeStruct((tokens + 2 * top, width), BF16),
        [pl.BlockSpec()] * 3,
        0,
        1 << 18,
    )(grad_out, ids, gates)
    blocks = [across(block, False, rel) for rel in range(4)]
    ws = lax.all_gather(w_down[0], "y", axis=0, tiled=True)

    picked = call(
        functools.partial(select_kernel, tokens, top, cap),
        jax.ShapeDtypeStruct((16, cap, 4 * width), BF16),
        [smem] + [vmem] * 4,
        2 * sources * cap * tokens * width,
        3 * sources * cap * width,
    )(at, *blocks)
    rows = lax.all_to_all(picked, group_of, split_axis=0, concat_axis=0, tiled=True)
    rows = rows.reshape(slots, 4 * width)

    a, b = call(
        project_kernel,
        [jax.ShapeDtypeStruct((4, slots // 4, hidden // 2), BF16)] * 2,
        [smem] + [vmem] * 2,
        8 * slots * width * hidden,
        8 * slots * width,
    )(at, rows, ws)
    acts = hidden_slots.reshape(4, 4, slots // 4, hidden)
    gate_part = call(
        gate_kernel,
        jax.ShapeDtypeStruct((4, slots // 4), F32),
        [smem] + [vmem] * 3,
        2 * slots * hidden,
        4 * slots * hidden,
    )(at, a, b, acts)
    part = call(
        weights_kernel,
        jax.ShapeDtypeStruct((4 * width, hidden), BF16),
        [smem] + [vmem] * 2,
        8 * slots * width * hidden,
        8 * slots * width,
    )(at, rows, acts)
    d_wdown = lax.psum_scatter(part, "y", scatter_dimension=0, tiled=True)

    returned = lax.all_to_all(
        gate_part.reshape(16, cap), group_of, split_axis=0, concat_axis=0, tiled=True
    )
    d_gate, rider = call(
        route_kernel,
        [jax.ShapeDtypeStruct((top, tokens), F32), jax.ShapeDtypeStruct((16, 3 * tokens), BF16)],
        [smem] + [vmem] * 6,
        1 << 20,
        1 << 16,
    )(at, ids, gates, *[across(returned, True, rel) for rel in range(4)])

    rows_of = slots // 4
    a2 = shift(jnp.concatenate([a[2], rider]), "zh", 1)
    b2 = shift(jnp.concatenate([b[2], rider]), "zh", -1)
    b1, a3 = shift(b[1], "zh", 1), shift(a[3], "zh", -1)
    a1 = add(a[1], a2[:rows_of]).astype(BF16)
    a1 = shift(jnp.concatenate([a1, a2[rows_of:]]), "zh", 1)
    b3 = shift(add(b[3], b2[:rows_of]).astype(BF16), "zh", -1)
    u = jnp.concatenate([add(a[0], a1[:rows_of], a3), add(b[0], b3, b1)], axis=1)
    d_hidden = u.astype(BF16).reshape(1, 4, cap, hidden)
    riders = add(a2[rows_of:], b2[rows_of:], a1[rows_of:])
    d_gate = d_gate + riders[:top, :tokens] + riders[:top, tokens : 2 * tokens]
    return d_hidden, d_gate.T, d_wdown[None]


def solution(mesh):
    fine = Mesh(mesh.devices.reshape(4, 4, 4, 2, 2, 2, 2), ("zh", "y") + EXPERT)
    dp = ("zh", "y")
    return jax.shard_map(
        on_device,
        mesh=fine,
        in_specs=(
            P(EXPERT, dp),
            P(EXPERT, None),
            P(EXPERT, None),
            P(EXPERT, dp, None),
            P(EXPERT, None, None, None),
        ),
        out_specs=(P(EXPERT, dp, None, None), P(EXPERT, None), P(EXPERT, dp, None)),
        check_vma=False,
    )
```

```python
import functools

import jax
import jax.numpy as jnp
from jax import lax
from jax.experimental import pallas as pl
from jax.experimental.pallas import tpu as pltpu
from jax.sharding import Mesh
from jax.sharding import PartitionSpec as P

BF16 = jnp.bfloat16
F32 = jnp.float32
EXPERT = ("x", "b2", "b1", "b0", "c")
VMEM_LIMIT = 16 * 1024 * 1024


def call(kernel, outs, in_specs, flops, moved):
    return pl.pallas_call(
        kernel,
        out_shape=outs,
        in_specs=in_specs,
        out_specs=jax.tree.map(lambda _: pl.BlockSpec(memory_space=pltpu.VMEM), outs),
        compiler_params=pltpu.CompilerParams(vmem_limit_bytes=VMEM_LIMIT),
        cost_estimate=pl.CostEstimate(flops=flops, bytes_accessed=moved, transcendentals=0),
    )


def iota(shape, dim):
    return lax.broadcasted_iota(jnp.int32, shape, dim)


def places(ids, experts):
    tokens = ids.shape[1]
    named = jnp.zeros((experts.shape[0], tokens), F32)
    for k in range(ids.shape[0]):
        named = jnp.where(ids[k : k + 1, :] == experts, 1.0, named)
    earlier = (iota((tokens, tokens), 0) < iota((tokens, tokens), 1)).astype(F32)
    before = jnp.dot(named.astype(BF16), earlier.astype(BF16), preferred_element_type=F32)
    return jnp.where(named > 0.0, before.astype(jnp.int32), -1)


def group(near, shape):
    d = iota(shape, 0)
    return (d // 4) * 16 + near * 4 + d % 4


def pack_kernel(grad_ref, ids_ref, gates_ref, out_ref):
    tokens = grad_ref.shape[0]
    ids = ids_ref[...].astype(F32)
    gates = gates_ref[...]
    high = gates.astype(BF16).astype(F32)
    out_ref[:tokens, :] = grad_ref[...]
    left = jnp.concatenate([ids, ids], axis=0)
    right = jnp.concatenate([high, gates - high], axis=0)
    out_ref[tokens:, :] = jnp.concatenate([left, right], axis=1).astype(BF16)


def select_kernel(tokens, top, cap, at_ref, *refs):
    blocks, out_ref = refs[:-1], refs[-1]
    near = at_ref[0]
    dests = out_ref.shape[0] // len(blocks)
    experts = group(near, (dests, tokens))
    slot = iota((cap, tokens), 0)
    for rel, block in enumerate(blocks):
        below = block[tokens : tokens + 2 * top, :].astype(F32)
        ids = below[:top, :tokens].astype(jnp.int32)
        gates = below[:top, tokens : 2 * tokens] + below[top:, tokens : 2 * tokens]
        place = places(ids, experts)
        weight = jnp.zeros((dests, tokens), F32)
        for k in range(top):
            weight = jnp.where(ids[k : k + 1, :] == experts, gates[k : k + 1, :], weight)
        picks, scales = [], []
        for i in range(dests):
            hit = place[i : i + 1, :] == slot
            picks.append(jnp.where(hit, 1.0, 0.0))
            scales.append(jnp.sum(jnp.where(hit, weight[i : i + 1, :], 0.0), axis=1, keepdims=True))
        picks = jnp.concatenate(picks, axis=0).astype(BF16)
        picked = jnp.dot(picks, block[:tokens, :], preferred_element_type=F32)
        index = jnp.bitwise_xor(near, rel)
        for i in range(dests):
            rows = picked[i * cap : (i + 1) * cap, :] * scales[i]
            out_ref[i * len(blocks) + index] = rows.astype(BF16)


def split(value):
    high = value.astype(BF16).astype(F32)
    return jnp.concatenate([high, value - high], axis=1)


def joined(rider):
    half = rider.shape[1] // 2
    rider = rider[:4].astype(F32)
    return rider[:, :half] + rider[:, half:]


def padded(rider):
    return jnp.concatenate([rider, jnp.zeros((12, rider.shape[1]), F32)], axis=0).astype(BF16)


def project_kernel(at_ref, rows_ref, w_ref, acts_ref, *outs):
    y, zh, way = at_ref[1], at_ref[2], at_ref[3]
    w = w_ref[...]
    ones = jnp.ones((8, w.shape[1]), F32)
    share = rows_ref.shape[2]
    lines = []
    pieces = rows_ref.shape[0]
    for r in range(pieces):
        mine = (y + way * r) % pieces
        piece = rows_ref[mine].reshape(4 * share, -1)
        u = jnp.dot(piece, w, preferred_element_type=F32)
        product = u * acts_ref[:, mine].reshape(4 * share, -1).astype(F32)
        line = lax.dot_general(
            ones,
            product,
            (((1,), (1,)), ((), ())),
            precision=lax.Precision.HIGHEST,
            preferred_element_type=F32,
        )
        lines.append((mine, line[0:1, :]))
        u = u.astype(BF16)
        for x in range(4):
            far = (way * (x - zh) + 4) % 4
            at = pl.ds(pl.multiple_of(far * share, share), share)
            outs[r][at, :] = u[x * share : (x + 1) * share, :]
    row = iota((4, 4 * share), 0)
    found = jnp.zeros((4, 4 * share), F32)
    for mine, line in lines:
        found = jnp.where(row == mine, line, found)
    outs[3][4 * share :, :] = padded(split(found))


def turn_kernel(own_ref, sent_ref, one_ref, two_ref, three_ref, *outs):
    rows = own_ref.shape[0]
    share = rows // 4
    riders = [ref[rows:, :] for ref in (sent_ref, one_ref, two_ref, three_ref)]
    gates = joined(riders[0]) + joined(riders[1]) + joined(riders[2]) + joined(riders[3])
    for r in range(4):
        at = slice(r * share, (r + 1) * share)
        u = own_ref[at, :].astype(F32) + three_ref[at, :].astype(F32)
        outs[r][:share, :] = u.astype(BF16)
    outs[3][share:, :] = padded(split(gates))


def finish_kernel(own_ref, sent_ref, one_ref, two_ref, three_ref, out_ref, gate_ref):
    rows = own_ref.shape[0]
    out_ref[...] = (own_ref[...].astype(F32) + three_ref[:rows, :].astype(F32)).astype(BF16)
    riders = [ref[rows:, :] for ref in (sent_ref, one_ref, two_ref, three_ref)]
    gate_ref[...] = joined(riders[0]) + joined(riders[1]) + joined(riders[2]) + joined(riders[3])


def pass_kernel(own_ref, came_ref, out_ref):
    rows = own_ref.shape[0]
    out_ref[:rows, :] = (own_ref[...].astype(F32) + came_ref[:rows, :].astype(F32)).astype(BF16)
    out_ref[rows:, :] = came_ref[rows:, :]


def weights_kernel(rows_ref, acts_ref, out_ref):
    total = jnp.zeros(out_ref.shape, F32)
    for y in range(rows_ref.shape[0]):
        piece = rows_ref[y].reshape(-1, rows_ref.shape[3])
        acts = acts_ref[:, y].reshape(piece.shape[0], -1)
        total = total + lax.dot_general(
            piece, acts, (((0,), (0,)), ((), ())), preferred_element_type=F32
        )
    out_ref[...] = total.astype(BF16)


def route_kernel(ids_ref, gates_ref, returned_ref, out_ref):
    ids, gates = ids_ref[...], gates_ref[...]
    experts, cap = returned_ref.shape
    tokens = ids.shape[1]
    e = iota((experts, tokens), 0)
    place = places(ids, e)
    returned = returned_ref[...]
    found = jnp.zeros((experts, tokens), F32)
    for p in range(cap):
        found = jnp.where(place == p, returned[:, p : p + 1], found)
    for k in range(ids.shape[0]):
        mine = jnp.where(ids[k : k + 1, :] == e, found, 0.0)
        out_ref[k : k + 1, :] = jnp.sum(mine, axis=0, keepdims=True) / gates[k : k + 1, :]


def swap(value, axis, bit=1):
    return lax.ppermute(value, axis, [(i, i ^ bit) for i in range(lax.axis_size(axis))])


def step(value, axis):
    size = lax.axis_size(axis)
    pairs = [
        (i * 2 + c, (i + 1 - 2 * c) % size * 2 + c) for i in range(size) for c in range(2)
    ]
    return lax.ppermute(value, (axis, "c"), pairs)


def passed(own, came):
    return call(
        pass_kernel,
        jax.ShapeDtypeStruct(came.shape, BF16),
        [pl.BlockSpec(memory_space=pltpu.VMEM)] * 2,
        own.size,
        6 * own.size,
    )(own, came)


def on_device(grad_out, expert_ids, gate_values, w_down, hidden_slots):
    tokens, width = grad_out.shape
    top = expert_ids.shape[1]
    _, sources, cap, hidden = hidden_slots.shape
    near = lax.axis_index("b2") * 2 + lax.axis_index("b1")
    way = 1 - 2 * lax.axis_index("c")
    at = jnp.stack([near, lax.axis_index("y"), lax.axis_index("zh"), way]).astype(jnp.int32)
    smem = pl.BlockSpec(memory_space=pltpu.SMEM)
    vmem = pl.BlockSpec(memory_space=pltpu.VMEM)
    ids, gates = expert_ids.T, gate_values.T
    slots = sources * cap
    share = slots // 16
    rider = 16

    def array(rows, columns=hidden):
        return jax.ShapeDtypeStruct((rows, columns), BF16)

    block = call(
        pack_kernel, array(tokens + 2 * top, width), [pl.BlockSpec()] * 3, 0, 1 << 18
    )(grad_out, ids, gates)
    over_b1 = swap(block, "b1")
    over_b2 = swap(block, "b2")
    over_both = swap(over_b2, "b1")
    picked = call(
        functools.partial(select_kernel, tokens, top, cap),
        jax.ShapeDtypeStruct((sources, cap, width), BF16),
        [smem] + [vmem] * 4,
        2 * slots * tokens * width,
        3 * slots * width,
    )(at, block, over_b1, over_b2, over_both)
    rows = lax.all_to_all(
        picked.reshape(16, 4, cap, width), ("x", "b0", "c"), split_axis=0, concat_axis=0, tiled=True
    )
    rows = rows.reshape(4, 4, 4, cap, width).transpose(2, 0, 1, 3, 4).reshape(4, 4, share, width)
    acts = hidden_slots.reshape(4, 4, share, hidden)

    piece = 4 * share
    u = call(
        project_kernel,
        [array(piece), array(piece), array(piece), array(piece + rider)],
        [smem] + [vmem] * 3,
        2 * slots * width * hidden,
        2 * slots * (width + hidden),
    )(at, rows, w_down[0], acts)
    one = step(u[3], "y")
    two = step(passed(u[2], one), "y")
    three = step(passed(u[1], two), "y")
    v = call(
        turn_kernel,
        [array(share), array(share), array(share), array(share + rider)],
        [vmem] * 5,
        piece * hidden,
        6 * piece * hidden,
    )(u[0], u[3], one, two, three)
    one = step(v[3], "zh")
    two = step(passed(v[2], one), "zh")
    three = step(passed(v[1], two), "zh")
    d_hidden, slot_gate = call(
        finish_kernel,
        [array(share), jax.ShapeDtypeStruct((4, 4 * share), F32)],
        [vmem] * 5,
        share * hidden,
        6 * share * hidden,
    )(v[0], v[3], one, two, three)

    slot_gate = slot_gate.reshape(4, 4, share).transpose(1, 0, 2).reshape(sources, cap)
    returned = lax.all_to_all(slot_gate, EXPERT, split_axis=0, concat_axis=0, tiled=True)
    d_gate = call(
        route_kernel, jax.ShapeDtypeStruct((top, tokens), F32), [vmem] * 3, 1 << 20, 1 << 16
    )(ids, gates, returned)
    d_wdown = call(
        weights_kernel,
        array(width),
        [vmem] * 2,
        2 * slots * width * hidden,
        2 * slots * (width + hidden),
    )(rows, acts)
    return d_hidden.reshape(1, 4, cap, hidden), d_gate.T, d_wdown[None]


def solution(mesh):
    fine = Mesh(mesh.devices.reshape(4, 4, 4, 2, 2, 2, 2), ("zh", "y") + EXPERT)
    dp = ("zh", "y")
    return jax.shard_map(
        on_device,
        mesh=fine,
        in_specs=(
            P(EXPERT, dp),
            P(EXPERT, None),
            P(EXPERT, None),
            P(EXPERT, dp, None),
            P(EXPERT, None, None, None),
        ),
        out_specs=(P(EXPERT, dp, None, None), P(EXPERT, None), P(EXPERT, dp, None)),
        check_vma=False,
    )
```

```python
import functools

import jax
import jax.numpy as jnp
from jax import lax
from jax.experimental import pallas as pl
from jax.experimental.pallas import tpu as pltpu
from jax.sharding import Mesh
from jax.sharding import PartitionSpec as P

BF16 = jnp.bfloat16
F32 = jnp.float32
EXPERT = ("x", "b2", "b1", "b0", "c")
VMEM_LIMIT = 16 * 1024 * 1024


def call(kernel, outs, in_specs, flops, moved):
    return pl.pallas_call(
        kernel,
        out_shape=outs,
        in_specs=in_specs,
        out_specs=jax.tree.map(lambda _: pl.BlockSpec(memory_space=pltpu.VMEM), outs),
        compiler_params=pltpu.CompilerParams(vmem_limit_bytes=VMEM_LIMIT),
        cost_estimate=pl.CostEstimate(flops=flops, bytes_accessed=moved, transcendentals=0),
    )


def iota(shape, dim):
    return lax.broadcasted_iota(jnp.int32, shape, dim)


def places(ids, experts):
    tokens = ids.shape[1]
    named = jnp.zeros((experts.shape[0], tokens), F32)
    for k in range(ids.shape[0]):
        named = jnp.where(ids[k : k + 1, :] == experts, 1.0, named)
    earlier = (iota((tokens, tokens), 0) < iota((tokens, tokens), 1)).astype(F32)
    before = jnp.dot(named.astype(BF16), earlier.astype(BF16), preferred_element_type=F32)
    return jnp.where(named > 0.0, before.astype(jnp.int32), -1)


def group(near, shape):
    d = iota(shape, 0)
    return (d // 4) * 16 + near * 4 + d % 4


def pack_kernel(grad_hbm, ids_hbm, gates_hbm, out_ref, ids_ref, gates_ref, sems):
    tokens = grad_hbm.shape[0]
    copies = [
        pltpu.make_async_copy(ids_hbm, ids_ref, sems.at[0]),
        pltpu.make_async_copy(gates_hbm, gates_ref, sems.at[1]),
        pltpu.make_async_copy(grad_hbm, out_ref.at[pl.ds(0, tokens)], sems.at[2]),
    ]
    for copy in copies:
        copy.start()
    copies[0].wait()
    copies[1].wait()
    ids = ids_ref[...].astype(F32)
    gates = gates_ref[...]
    high = gates.astype(BF16).astype(F32)
    left = jnp.concatenate([ids, ids], axis=0)
    right = jnp.concatenate([high, gates - high], axis=0)
    out_ref[tokens:, :] = jnp.concatenate([left, right], axis=1).astype(BF16)
    copies[2].wait()


def select_kernel(tokens, top, cap, at_ref, *refs):
    blocks, out_ref = refs[:-1], refs[-1]
    near = at_ref[0]
    dests = out_ref.shape[0] // len(blocks)
    experts = group(near, (dests, tokens))
    slot = iota((cap, tokens), 0)
    for rel, block in enumerate(blocks):
        below = block[tokens : tokens + 2 * top, :].astype(F32)
        ids = below[:top, :tokens].astype(jnp.int32)
        gates = below[:top, tokens : 2 * tokens] + below[top:, tokens : 2 * tokens]
        place = places(ids, experts)
        weight = jnp.zeros((dests, tokens), F32)
        for k in range(top):
            weight = jnp.where(ids[k : k + 1, :] == experts, gates[k : k + 1, :], weight)
        picks, scales = [], []
        for i in range(dests):
            hit = place[i : i + 1, :] == slot
            picks.append(jnp.where(hit, 1.0, 0.0))
            scales.append(jnp.sum(jnp.where(hit, weight[i : i + 1, :], 0.0), axis=1, keepdims=True))
        picks = jnp.concatenate(picks, axis=0).astype(BF16)
        picked = jnp.dot(picks, block[:tokens, :], preferred_element_type=F32)
        index = jnp.bitwise_xor(near, rel)
        for i in range(dests):
            rows = picked[i * cap : (i + 1) * cap, :] * scales[i]
            out_ref[i * len(blocks) + index] = rows.astype(BF16)


def split(value):
    high = value.astype(BF16).astype(F32)
    return jnp.concatenate([high, value - high], axis=1)


def joined(rider):
    half = rider.shape[1] // 2
    rider = rider[:4].astype(F32)
    return rider[:, :half] + rider[:, half:]


def padded(rider):
    return jnp.concatenate([rider, jnp.zeros((12, rider.shape[1]), F32)], axis=0).astype(BF16)


def project_kernel(at_ref, rows_ref, w_ref, acts_ref, *outs):
    y, zh, way = at_ref[1], at_ref[2], at_ref[3]
    w = w_ref[...]
    ones = jnp.ones((8, 128), F32)
    share = rows_ref.shape[2]
    pieces = rows_ref.shape[0]
    row = iota((4, 4 * share), 0)
    found = jnp.zeros((4, 4 * share), F32)
    for r in range(pieces):
        mine = (y + way * r) % pieces
        piece = rows_ref[mine].reshape(4 * share, -1)
        u = jnp.dot(piece, w, preferred_element_type=F32)
        product = u * acts_ref[:, mine].reshape(4 * share, -1).astype(F32)
        product = sum(product[:, k : k + 128] for k in range(0, w.shape[1], 128))
        line = lax.dot_general(
            ones,
            product,
            (((1,), (1,)), ((), ())),
            precision=lax.Precision.HIGHEST,
            preferred_element_type=F32,
        )
        found = jnp.where(row == mine, line[0:1, :], found)
        u = u.astype(BF16)
        for x in range(4):
            far = (way * (x - zh) + 4) % 4
            at = pl.ds(pl.multiple_of(far * share, share), share)
            outs[r][at, :] = u[x * share : (x + 1) * share, :]
    rider = padded(split(found))
    for r in range(1, 4):
        outs[r][4 * share :, :] = rider


def turn_kernel(own_ref, sent_ref, one_ref, two_ref, three_ref, *outs):
    rows = own_ref.shape[0]
    share = rows // 4
    came = (one_ref, two_ref, three_ref)
    gates = joined(sent_ref[rows:, :])
    for ref in came:
        gates = gates + joined(ref[rows:, :])
    rider = padded(split(gates))
    for r in range(4):
        at = slice(r * share, (r + 1) * share)
        u = own_ref[at, :].astype(F32)
        for ref in came:
            u = u + ref[at, :].astype(F32)
        outs[r][:share, :] = u.astype(BF16)
        if r > 0:
            outs[r][share:, :] = rider


def finish_kernel(own_ref, sent_ref, one_ref, two_ref, three_ref, out_ref, gate_ref):
    rows = own_ref.shape[0]
    u = own_ref[...].astype(F32)
    gates = joined(sent_ref[rows:, :])
    for ref in (one_ref, two_ref, three_ref):
        u = u + ref[:rows, :].astype(F32)
        gates = gates + joined(ref[rows:, :])
    out_ref[...] = u.astype(BF16)
    gate_ref[...] = gates


def weights_kernel(rows_ref, acts_ref, out_ref):
    total = jnp.zeros(out_ref.shape, F32)
    for y in range(rows_ref.shape[0]):
        piece = rows_ref[y].reshape(-1, rows_ref.shape[3])
        acts = acts_ref[:, y].reshape(piece.shape[0], -1)
        total = total + lax.dot_general(
            piece, acts, (((0,), (0,)), ((), ())), preferred_element_type=F32
        )
    out_ref[...] = total.astype(BF16)


def route_kernel(ids_ref, gates_ref, returned_ref, out_ref):
    ids, gates = ids_ref[...], gates_ref[...]
    experts, cap = returned_ref.shape
    tokens = ids.shape[1]
    e = iota((experts, tokens), 0)
    place = places(ids, e)
    returned = returned_ref[...]
    found = jnp.zeros((experts, tokens), F32)
    for p in range(cap):
        found = jnp.where(place == p, returned[:, p : p + 1], found)
    for k in range(ids.shape[0]):
        mine = jnp.where(ids[k : k + 1, :] == e, found, 0.0)
        out_ref[k : k + 1, :] = jnp.sum(mine, axis=0, keepdims=True) / gates[k : k + 1, :]


def ahead(value, axis, by):
    pairs = [(i * 2 + c, (i + (1 - 2 * c) * by) % 4 * 2 + c) for i in range(4) for c in range(2)]
    return lax.ppermute(value, (axis, "c"), pairs)


def on_device(grad_out, expert_ids, gate_values, w_down, hidden_slots):
    tokens, width = grad_out.shape
    top = expert_ids.shape[1]
    _, sources, cap, hidden = hidden_slots.shape
    near = lax.axis_index("b2") * 2 + lax.axis_index("b1")
    way = 1 - 2 * lax.axis_index("c")
    at = jnp.stack([near, lax.axis_index("y"), lax.axis_index("zh"), way]).astype(jnp.int32)
    smem = pl.BlockSpec(memory_space=pltpu.SMEM)
    vmem = pl.BlockSpec(memory_space=pltpu.VMEM)
    ids, gates = expert_ids.T, gate_values.T
    slots = sources * cap
    share = slots // 16
    rider = 16

    def array(rows, columns=hidden):
        return jax.ShapeDtypeStruct((rows, columns), BF16)

    block = pl.pallas_call(
        pack_kernel,
        out_shape=array(tokens + 2 * top, width),
        in_specs=[pl.BlockSpec(memory_space=pltpu.HBM)] * 3,
        out_specs=vmem,
        scratch_shapes=[
            pltpu.VMEM((top, tokens), jnp.int32),
            pltpu.VMEM((top, tokens), F32),
            pltpu.SemaphoreType.DMA((3,)),
        ],
        compiler_params=pltpu.CompilerParams(vmem_limit_bytes=VMEM_LIMIT),
        cost_estimate=pl.CostEstimate(flops=0, bytes_accessed=1 << 18, transcendentals=0),
    )(grad_out, ids, gates)
    others = [lax.ppermute(block, ("b2", "b1"), [(i, i ^ rel) for i in range(4)]) for rel in (1, 2, 3)]
    picked = call(
        functools.partial(select_kernel, tokens, top, cap),
        jax.ShapeDtypeStruct((sources, cap, width), BF16),
        [smem] + [vmem] * 4,
        2 * slots * tokens * width,
        3 * slots * width,
    )(at, block, *others)
    rows = lax.all_to_all(
        picked.reshape(16, 4, cap, width), ("x", "b0", "c"), split_axis=0, concat_axis=0, tiled=True
    )
    rows = rows.reshape(4, 4, 4, cap, width).transpose(2, 0, 1, 3, 4).reshape(4, 4, share, width)
    acts = hidden_slots.reshape(4, 4, share, hidden)

    piece = 4 * share
    u = call(
        project_kernel,
        [array(piece)] + [array(piece + rider)] * 3,
        [smem] + [vmem] * 3,
        2 * slots * width * hidden,
        2 * slots * (width + hidden),
    )(at, rows, w_down[0], acts)
    came = [ahead(u[r], "y", r) for r in (1, 2, 3)]
    v = call(
        turn_kernel,
        [array(share)] + [array(share + rider)] * 3,
        [vmem] * 5,
        piece * hidden,
        6 * piece * hidden,
    )(u[0], u[1], *came)
    came = [ahead(v[r], "zh", r) for r in (1, 2, 3)]
    d_hidden, slot_gate = call(
        finish_kernel,
        [array(share), jax.ShapeDtypeStruct((4, 4 * share), F32)],
        [vmem] * 5,
        share * hidden,
        6 * share * hidden,
    )(v[0], v[1], *came)

    slot_gate = slot_gate.reshape(4, 4, share).transpose(1, 0, 2).reshape(sources, cap)
    returned = lax.all_to_all(slot_gate, EXPERT, split_axis=0, concat_axis=0, tiled=True)
    d_gate = call(
        route_kernel, jax.ShapeDtypeStruct((top, tokens), F32), [vmem] * 3, 1 << 20, 1 << 16
    )(ids, gates, returned)
    d_wdown = call(
        weights_kernel,
        array(width),
        [vmem] * 2,
        2 * slots * width * hidden,
        2 * slots * (width + hidden),
    )(rows, acts)
    return d_hidden.reshape(1, 4, cap, hidden), d_gate.T, d_wdown[None]


def solution(mesh):
    fine = Mesh(mesh.devices.reshape(4, 4, 4, 2, 2, 2, 2), ("zh", "y") + EXPERT)
    dp = ("zh", "y")
    return jax.shard_map(
        on_device,
        mesh=fine,
        in_specs=(
            P(EXPERT, dp),
            P(EXPERT, None),
            P(EXPERT, None),
            P(EXPERT, dp, None),
            P(EXPERT, None, None, None),
        ),
        out_specs=(P(EXPERT, dp, None, None), P(EXPERT, None), P(EXPERT, dp, None)),
        check_vma=False,
    )
```

```python
import functools

import jax
import jax.numpy as jnp
from jax import lax
from jax.experimental import pallas as pl
from jax.experimental.pallas import tpu as pltpu
from jax.sharding import Mesh
from jax.sharding import PartitionSpec as P

BF16 = jnp.bfloat16
F32 = jnp.float32
EXPERT = ("x", "b2", "b1", "b0", "c")
VMEM_LIMIT = 16 * 1024 * 1024


def call(kernel, outs, in_specs, flops, moved):
    return pl.pallas_call(
        kernel,
        out_shape=outs,
        in_specs=in_specs,
        out_specs=jax.tree.map(lambda _: pl.BlockSpec(memory_space=pltpu.VMEM), outs),
        compiler_params=pltpu.CompilerParams(vmem_limit_bytes=VMEM_LIMIT),
        cost_estimate=pl.CostEstimate(flops=flops, bytes_accessed=moved, transcendentals=0),
    )


def iota(shape, dim):
    return lax.broadcasted_iota(jnp.int32, shape, dim)


def places(ids, experts):
    tokens = ids.shape[1]
    named = jnp.zeros((experts.shape[0], tokens), F32)
    for k in range(ids.shape[0]):
        named = jnp.where(ids[k : k + 1, :] == experts, 1.0, named)
    earlier = (iota((tokens, tokens), 0) < iota((tokens, tokens), 1)).astype(F32)
    before = jnp.dot(named.astype(BF16), earlier.astype(BF16), preferred_element_type=F32)
    return jnp.where(named > 0.0, before.astype(jnp.int32), -1)


def group(near, shape):
    d = iota(shape, 0)
    return (d // 4) * 16 + near * 4 + d % 4


def pack_kernel(grad_hbm, ids_hbm, gates_hbm, out_ref, ids_ref, gates_ref, sems):
    tokens = grad_hbm.shape[0]
    copies = [
        pltpu.make_async_copy(ids_hbm, ids_ref, sems.at[0]),
        pltpu.make_async_copy(gates_hbm, gates_ref, sems.at[1]),
        pltpu.make_async_copy(grad_hbm, out_ref.at[pl.ds(0, tokens)], sems.at[2]),
    ]
    for copy in copies:
        copy.start()
    copies[0].wait()
    copies[1].wait()
    ids = ids_ref[...].astype(F32)
    gates = gates_ref[...]
    high = gates.astype(BF16).astype(F32)
    left = jnp.concatenate([ids, ids], axis=0)
    right = jnp.concatenate([high, gates - high], axis=0)
    out_ref[tokens:, :] = jnp.concatenate([left, right], axis=1).astype(BF16)
    copies[2].wait()


def select_kernel(tokens, top, cap, at_ref, *refs):
    blocks, out_ref = refs[:-1], refs[-1]
    near = at_ref[0]
    dests = out_ref.shape[0] // len(blocks)
    experts = group(near, (dests, tokens))
    slot = iota((cap, tokens), 0)
    for rel, block in enumerate(blocks):
        below = block[tokens : tokens + 2 * top, :].astype(F32)
        ids = below[:top, :tokens].astype(jnp.int32)
        gates = below[:top, tokens : 2 * tokens] + below[top:, tokens : 2 * tokens]
        place = places(ids, experts)
        weight = jnp.zeros((dests, tokens), F32)
        for k in range(top):
            weight = jnp.where(ids[k : k + 1, :] == experts, gates[k : k + 1, :], weight)
        picks, scales = [], []
        for i in range(dests):
            hit = place[i : i + 1, :] == slot
            picks.append(jnp.where(hit, 1.0, 0.0))
            scales.append(jnp.sum(jnp.where(hit, weight[i : i + 1, :], 0.0), axis=1, keepdims=True))
        picks = jnp.concatenate(picks, axis=0).astype(BF16)
        picked = jnp.dot(picks, block[:tokens, :], preferred_element_type=F32)
        index = jnp.bitwise_xor(near, rel)
        for i in range(dests):
            rows = picked[i * cap : (i + 1) * cap, :] * scales[i]
            out_ref[i * len(blocks) + index] = rows.astype(BF16)


def riding(part):
    high = part.astype(BF16).astype(F32)
    rider = jnp.concatenate([high, part - high], axis=1)
    return jnp.concatenate([rider, jnp.zeros((12, rider.shape[1]), F32)], axis=0).astype(BF16)


def ridden(rider):
    part = rider[:4].astype(F32)
    half = part.shape[1] // 2
    return part[:, :half] + part[:, half:]


def project_kernel(at_ref, rows_ref, w_ref, acts_ref, rider_ref, *outs):
    y, zh, way = at_ref[1], at_ref[2], at_ref[3]
    w = w_ref[...]
    ones = jnp.ones((8, 128), F32)
    share = rows_ref.shape[2]
    pieces = rows_ref.shape[0]
    row = iota((pieces, 4 * share), 0)
    gates = jnp.zeros((pieces, 4 * share), F32)
    for r in range(pieces):
        mine = (y + way * r) % pieces
        piece = rows_ref[mine].reshape(4 * share, -1)
        u = jnp.dot(piece, w, preferred_element_type=F32)
        product = u * acts_ref[:, mine].reshape(4 * share, -1).astype(F32)
        product = sum(product[:, k : k + 128] for k in range(0, w.shape[1], 128))
        line = lax.dot_general(
            ones,
            product,
            (((1,), (1,)), ((), ())),
            precision=lax.Precision.HIGHEST,
            preferred_element_type=F32,
        )
        gates = jnp.where(row == mine, line[0:1, :], gates)
        u = u.astype(BF16)
        for x in range(4):
            far = (way * (x - zh) + 4) % 4
            part = u[x * share : (x + 1) * share, :]

            @pl.when(far == 2)
            def _():
                outs[r][...] = part

            @pl.when(far != 2)
            def _():
                place = far // 2
                place = jnp.where(far == 0, 2, place)
                at = pl.ds(pl.multiple_of(place * share, share), share)
                outs[4 + r][at, :] = part

    rider = riding(gates)
    rider_ref[...] = rider
    for r in range(1, pieces):
        outs[4 + r][3 * share :, :] = rider


def first_kernel(own_ref, one_ref, two_ref, three_ref, a_ref, b_ref):
    half = a_ref.shape[1]
    u = own_ref[...].astype(F32)
    for ref in (one_ref, two_ref, three_ref):
        u = u + ref[...].astype(F32)
    a_ref[...] = u[:, :half].astype(BF16)
    b_ref[...] = u[:, half:].astype(BF16)


def second_kernel(own_ref, rider_ref, one_ref, two_ref, three_ref, a_ref, b_ref, *outs):
    share, half = a_ref.shape
    ahead_ref, behind_ref, mine_ref, gates_ref = outs
    came = (one_ref, two_ref, three_ref)

    def total(k):
        at = slice(k * share, (k + 1) * share)
        u = own_ref[at, :].astype(F32)
        for ref in came:
            u = u + ref[at, :].astype(F32)
        return u

    gates = ridden(rider_ref[...])
    for ref in came:
        gates = gates + ridden(ref[3 * share :, :])
    rider = riding(gates)
    u = total(0)
    ahead_ref[:share, :half] = (u[:, :half] + a_ref[...].astype(F32)).astype(BF16)
    ahead_ref[:share, half:] = u[:, half:].astype(BF16)
    ahead_ref[share:, :] = rider
    u = total(1)
    behind_ref[:share, :half] = u[:, :half].astype(BF16)
    behind_ref[:share, half:] = (u[:, half:] + b_ref[...].astype(F32)).astype(BF16)
    behind_ref[share:, :] = rider
    mine_ref[...] = total(2).astype(BF16)
    gates_ref[...] = rider


def finish_kernel(own_ref, one_ref, three_ref, rider_ref, two_ref, out_ref, gate_ref):
    rows = own_ref.shape[0]
    u = own_ref[...].astype(F32)
    gates = ridden(rider_ref[...]) + ridden(two_ref[...])
    for ref in (one_ref, three_ref):
        u = u + ref[:rows, :].astype(F32)
        gates = gates + ridden(ref[rows:, :])
    out_ref[...] = u.astype(BF16)
    gate_ref[...] = gates


def weights_kernel(rows_ref, acts_ref, out_ref):
    total = jnp.zeros(out_ref.shape, F32)
    for y in range(rows_ref.shape[0]):
        piece = rows_ref[y].reshape(-1, rows_ref.shape[3])
        acts = acts_ref[:, y].reshape(piece.shape[0], -1)
        total = total + lax.dot_general(
            piece, acts, (((0,), (0,)), ((), ())), preferred_element_type=F32
        )
    out_ref[...] = total.astype(BF16)


def route_kernel(ids_ref, gates_ref, returned_ref, out_ref):
    ids, gates = ids_ref[...], gates_ref[...]
    experts, cap = returned_ref.shape
    tokens = ids.shape[1]
    e = iota((experts, tokens), 0)
    place = places(ids, e)
    returned = returned_ref[...]
    found = jnp.zeros((experts, tokens), F32)
    for p in range(cap):
        found = jnp.where(place == p, returned[:, p : p + 1], found)
    lines = []
    for k in range(ids.shape[0]):
        mine = jnp.where(ids[k : k + 1, :] == e, found, 0.0)
        lines.append(jnp.sum(mine, axis=0, keepdims=True))
    out_ref[...] = jnp.concatenate(lines, axis=0) / gates


def ahead(value, axis, by):
    pairs = [(i * 2 + c, (i + (1 - 2 * c) * by) % 4 * 2 + c) for i in range(4) for c in range(2)]
    return lax.ppermute(value, (axis, "c"), pairs)


def on_device(grad_out, expert_ids, gate_values, w_down, hidden_slots):
    tokens, width = grad_out.shape
    top = expert_ids.shape[1]
    _, sources, cap, hidden = hidden_slots.shape
    near = lax.axis_index("b2") * 2 + lax.axis_index("b1")
    way = 1 - 2 * lax.axis_index("c")
    at = jnp.stack([near, lax.axis_index("y"), lax.axis_index("zh"), way]).astype(jnp.int32)
    smem = pl.BlockSpec(memory_space=pltpu.SMEM)
    vmem = pl.BlockSpec(memory_space=pltpu.VMEM)
    ids, gates = expert_ids.T, gate_values.T
    slots = sources * cap
    share = slots // 16
    rider = 16

    def array(rows, columns=hidden):
        return jax.ShapeDtypeStruct((rows, columns), BF16)

    block = pl.pallas_call(
        pack_kernel,
        out_shape=array(tokens + 2 * top, width),
        in_specs=[pl.BlockSpec(memory_space=pltpu.HBM)] * 3,
        out_specs=vmem,
        scratch_shapes=[
            pltpu.VMEM((top, tokens), jnp.int32),
            pltpu.VMEM((top, tokens), F32),
            pltpu.SemaphoreType.DMA((3,)),
        ],
        compiler_params=pltpu.CompilerParams(vmem_limit_bytes=VMEM_LIMIT),
        cost_estimate=pl.CostEstimate(flops=0, bytes_accessed=1 << 18, transcendentals=0),
    )(grad_out, ids, gates)
    others = [lax.ppermute(block, ("b2", "b1"), [(i, i ^ rel) for i in range(4)]) for rel in (1, 2, 3)]
    picked = call(
        functools.partial(select_kernel, tokens, top, cap),
        jax.ShapeDtypeStruct((sources, cap, width), BF16),
        [smem] + [vmem] * 4,
        2 * slots * tokens * width,
        3 * slots * width,
    )(at, block, *others)
    rows = lax.all_to_all(
        picked.reshape(16, 4, cap, width), ("x", "b0", "c"), split_axis=0, concat_axis=0, tiled=True
    )
    rows = rows.reshape(4, 4, 4, cap, width).transpose(2, 0, 1, 3, 4).reshape(4, 4, share, width)
    acts = hidden_slots.reshape(4, 4, share, hidden)

    rides, *u = call(
        project_kernel,
        [array(rider)] + [array(share)] * 4 + [array(3 * share)] + [array(3 * share + rider)] * 3,
        [smem] + [vmem] * 3,
        2 * slots * width * hidden,
        2 * slots * (width + hidden),
    )(at, rows, w_down[0], acts)
    came = [ahead(u[r], "y", r) for r in (1, 2, 3)]
    came, u = lax.optimization_barrier((came, u))
    a, b = call(
        first_kernel,
        [array(share, hidden // 2)] * 2,
        [vmem] * 4,
        4 * share * hidden,
        10 * share * hidden,
    )(u[0], *came)
    a, b = ahead(a, "zh", 1), ahead(b, "zh", -1)
    came = [ahead(u[4 + r], "y", r) for r in (1, 2, 3)]

    one, three, own, rides = call(
        second_kernel,
        [array(share + rider)] * 2 + [array(share), array(rider)],
        [vmem] * 7,
        16 * share * hidden,
        32 * share * hidden,
    )(u[4], rides, *came, a, b)
    d_hidden, slot_gate = call(
        finish_kernel,
        [array(share), jax.ShapeDtypeStruct((4, 4 * share), F32)],
        [vmem] * 5,
        4 * share * hidden,
        8 * share * hidden,
    )(own, ahead(one, "zh", 1), ahead(three, "zh", -1), rides, ahead(rides, "zh", 2))
    slot_gate = slot_gate.reshape(4, 4, share).transpose(1, 0, 2).reshape(sources, cap)
    returned = lax.all_to_all(slot_gate, EXPERT, split_axis=0, concat_axis=0, tiled=True)
    d_gate = call(
        route_kernel, jax.ShapeDtypeStruct((top, tokens), F32), [vmem] * 3, 1 << 20, 1 << 16
    )(ids, gates, returned)
    d_wdown = call(
        weights_kernel,
        array(width),
        [vmem] * 2,
        2 * slots * width * hidden,
        2 * slots * (width + hidden),
    )(rows, acts)
    return d_hidden.reshape(1, 4, cap, hidden), d_gate.T, d_wdown[None]


def solution(mesh):
    fine = Mesh(mesh.devices.reshape(4, 4, 4, 2, 2, 2, 2), ("zh", "y") + EXPERT)
    dp = ("zh", "y")
    return jax.shard_map(
        on_device,
        mesh=fine,
        in_specs=(
            P(EXPERT, dp),
            P(EXPERT, None),
            P(EXPERT, None),
            P(EXPERT, dp, None),
            P(EXPERT, None, None, None),
        ),
        out_specs=(P(EXPERT, dp, None, None), P(EXPERT, None), P(EXPERT, dp, None)),
        check_vma=False,
    )
```

```python
import functools

import jax
import jax.numpy as jnp
from jax import lax
from jax.experimental import pallas as pl
from jax.experimental.pallas import tpu as pltpu
from jax.sharding import Mesh
from jax.sharding import PartitionSpec as P

BF16 = jnp.bfloat16
F32 = jnp.float32
EXPERT = ("x", "b2", "b1", "b0", "c")
VMEM_LIMIT = 16 * 1024 * 1024


def call(kernel, outs, in_specs, flops, moved):
    return pl.pallas_call(
        kernel,
        out_shape=outs,
        in_specs=in_specs,
        out_specs=jax.tree.map(lambda _: pl.BlockSpec(memory_space=pltpu.VMEM), outs),
        compiler_params=pltpu.CompilerParams(vmem_limit_bytes=VMEM_LIMIT),
        cost_estimate=pl.CostEstimate(flops=flops, bytes_accessed=moved, transcendentals=0),
    )


def iota(shape, dim):
    return lax.broadcasted_iota(jnp.int32, shape, dim)


def places(ids, experts):
    tokens = ids.shape[1]
    named = jnp.zeros((experts.shape[0], tokens), F32)
    for k in range(ids.shape[0]):
        named = jnp.where(ids[k : k + 1, :] == experts, 1.0, named)
    earlier = (iota((tokens, tokens), 0) < iota((tokens, tokens), 1)).astype(F32)
    before = jnp.dot(named.astype(BF16), earlier.astype(BF16), preferred_element_type=F32)
    return jnp.where(named > 0.0, before.astype(jnp.int32), -1)


def group(near, shape):
    d = iota(shape, 0)
    return (d // 4) * 16 + near * 4 + d % 4


def pack_kernel(grad_hbm, ids_hbm, gates_hbm, out_ref, ids_ref, gates_ref, sems):
    tokens = grad_hbm.shape[0]
    copies = [
        pltpu.make_async_copy(ids_hbm, ids_ref, sems.at[0]),
        pltpu.make_async_copy(gates_hbm, gates_ref, sems.at[1]),
        pltpu.make_async_copy(grad_hbm, out_ref.at[pl.ds(0, tokens)], sems.at[2]),
    ]
    for copy in copies:
        copy.start()
    copies[0].wait()
    copies[1].wait()
    ids = ids_ref[...].astype(F32)
    gates = gates_ref[...]
    high = gates.astype(BF16).astype(F32)
    left = jnp.concatenate([ids, ids], axis=0)
    right = jnp.concatenate([high, gates - high], axis=0)
    out_ref[tokens:, :] = jnp.concatenate([left, right], axis=1).astype(BF16)
    copies[2].wait()


def select_kernel(tokens, top, cap, at_ref, *refs):
    blocks, out_ref = refs[:-1], refs[-1]
    near = at_ref[0]
    dests = out_ref.shape[0] // len(blocks)
    experts = group(near, (dests, tokens))
    slot = iota((cap, tokens), 0)
    for rel, block in enumerate(blocks):
        below = block[tokens : tokens + 2 * top, :].astype(F32)
        ids = below[:top, :tokens].astype(jnp.int32)
        gates = below[:top, tokens : 2 * tokens] + below[top:, tokens : 2 * tokens]
        place = places(ids, experts)
        weight = jnp.zeros((dests, tokens), F32)
        for k in range(top):
            weight = jnp.where(ids[k : k + 1, :] == experts, gates[k : k + 1, :], weight)
        picks, scales = [], []
        for i in range(dests):
            hit = place[i : i + 1, :] == slot
            picks.append(jnp.where(hit, 1.0, 0.0))
            scales.append(jnp.sum(jnp.where(hit, weight[i : i + 1, :], 0.0), axis=1, keepdims=True))
        picks = jnp.concatenate(picks, axis=0).astype(BF16)
        picked = jnp.dot(picks, block[:tokens, :], preferred_element_type=F32)
        index = jnp.bitwise_xor(near, rel)
        for i in range(dests):
            rows = picked[i * cap : (i + 1) * cap, :] * scales[i]
            out_ref[i * len(blocks) + index] = rows.astype(BF16)


def riding(part):
    high = part.astype(BF16).astype(F32)
    rider = jnp.concatenate([high, part - high], axis=1)
    return jnp.concatenate([rider, jnp.zeros((12, rider.shape[1]), F32)], axis=0).astype(BF16)


def ridden(rider):
    part = rider[:4].astype(F32)
    half = part.shape[1] // 2
    return part[:, :half] + part[:, half:]


def riding_gates(part):
    high = part.astype(BF16).astype(F32)
    empty = jnp.zeros((part.shape[0], 4 * part.shape[1]), F32)
    rider = jnp.concatenate([high, part - high, empty], axis=1)
    return jnp.concatenate([rider, jnp.zeros_like(rider)], axis=0).astype(BF16)


def ridden_gates(rider):
    part = rider[:8, :256].astype(F32)
    return part[:, :128] + part[:, 128:]


def project_kernel(at_ref, rows_ref, w_ref, acts_ref, rider_ref, *outs):
    y, zh, way = at_ref[1], at_ref[2], at_ref[3]
    w = w_ref[...]
    ones = jnp.ones((8, 128), F32)
    share = rows_ref.shape[2]
    pieces = rows_ref.shape[0]
    row = iota((pieces, 4 * share), 0)
    gates = jnp.zeros((pieces, 4 * share), F32)
    for r in range(pieces):
        mine = (y + way * r) % pieces
        piece = rows_ref[mine].reshape(4 * share, -1)
        u = jnp.dot(piece, w, preferred_element_type=F32)
        product = u * acts_ref[:, mine].reshape(4 * share, -1).astype(F32)
        product = sum(product[:, k : k + 128] for k in range(0, w.shape[1], 128))
        line = lax.dot_general(
            ones,
            product,
            (((1,), (1,)), ((), ())),
            precision=lax.Precision.HIGHEST,
            preferred_element_type=F32,
        )
        gates = jnp.where(row == mine, line[0:1, :], gates)
        u = u.astype(BF16)
        for x in range(4):
            far = (way * (x - zh) + 4) % 4
            part = u[x * share : (x + 1) * share, :]

            @pl.when(far == 2)
            def _():
                outs[r][:share, :] = part

            @pl.when(far != 2)
            def _():
                place = far // 2
                place = jnp.where(far == 0, 2, place)
                at = pl.ds(pl.multiple_of(place * share, share), share)
                outs[4 + r][at, :] = part

    rider = riding(gates)
    rider_ref[...] = rider
    for r in range(1, pieces):
        outs[r][share:, :] = rider


def first_kernel(own_ref, rider_ref, one_ref, two_ref, three_ref, a_ref, b_ref, gate_ref):
    share, half = a_ref.shape
    u = own_ref[...].astype(F32)
    gates = ridden(rider_ref[...])
    for ref in (one_ref, two_ref, three_ref):
        u = u + ref[:share, :].astype(F32)
        gates = gates + ridden(ref[share:, :])
    a_ref[...] = u[:, :half].astype(BF16)
    b_ref[...] = u[:, half:].astype(BF16)
    gate_ref[...] = gates


def second_kernel(own_ref, gate_ref, one_ref, two_ref, three_ref, a_ref, b_ref, *outs):
    share, half = a_ref.shape
    ahead_ref, behind_ref, mine_ref, gates_ref = outs
    came = (one_ref, two_ref, three_ref)

    def total(k):
        at = slice(k * share, (k + 1) * share)
        u = own_ref[at, :].astype(F32)
        for ref in came:
            u = u + ref[at, :].astype(F32)
        return u

    rider = riding_gates(gate_ref[...])
    u = total(0)
    ahead_ref[:share, :half] = (u[:, :half] + a_ref[...].astype(F32)).astype(BF16)
    ahead_ref[:share, half:] = u[:, half:].astype(BF16)
    ahead_ref[share:, :] = rider
    u = total(1)
    behind_ref[:share, :half] = u[:, :half].astype(BF16)
    behind_ref[:share, half:] = (u[:, half:] + b_ref[...].astype(F32)).astype(BF16)
    behind_ref[share:, :] = rider
    mine_ref[...] = total(2).astype(BF16)
    gates_ref[...] = rider


def finish_kernel(own_ref, one_ref, three_ref, rider_ref, two_ref, out_ref, gate_ref):
    rows = own_ref.shape[0]
    u = own_ref[...].astype(F32)
    gates = ridden_gates(rider_ref[...]) + ridden_gates(two_ref[...])
    for ref in (one_ref, three_ref):
        u = u + ref[:rows, :].astype(F32)
        gates = gates + ridden_gates(ref[rows:, :])
    out_ref[...] = u.astype(BF16)
    gate_ref[...] = gates


def weights_kernel(rows_ref, acts_ref, out_ref):
    total = jnp.zeros(out_ref.shape, F32)
    for y in range(rows_ref.shape[0]):
        piece = rows_ref[y].reshape(-1, rows_ref.shape[3])
        acts = acts_ref[:, y].reshape(piece.shape[0], -1)
        total = total + lax.dot_general(
            piece, acts, (((0,), (0,)), ((), ())), preferred_element_type=F32
        )
    out_ref[...] = total.astype(BF16)


def route_kernel(ids_ref, gates_ref, returned_ref, out_ref):
    ids, gates = ids_ref[...], gates_ref[...]
    experts, cap = returned_ref.shape
    tokens = ids.shape[1]
    e = iota((experts, tokens), 0)
    place = places(ids, e)
    returned = returned_ref[...]
    found = jnp.zeros((experts, tokens), F32)
    for p in range(cap):
        found = jnp.where(place == p, returned[:, p : p + 1], found)
    lines = []
    for k in range(ids.shape[0]):
        mine = jnp.where(ids[k : k + 1, :] == e, found, 0.0)
        lines.append(jnp.sum(mine, axis=0, keepdims=True))
    out_ref[...] = jnp.concatenate(lines, axis=0) / gates


def ahead(value, axis, by):
    pairs = [(i * 2 + c, (i + (1 - 2 * c) * by) % 4 * 2 + c) for i in range(4) for c in range(2)]
    return lax.ppermute(value, (axis, "c"), pairs)


def on_device(grad_out, expert_ids, gate_values, w_down, hidden_slots):
    tokens, width = grad_out.shape
    top = expert_ids.shape[1]
    _, sources, cap, hidden = hidden_slots.shape
    near = lax.axis_index("b2") * 2 + lax.axis_index("b1")
    way = 1 - 2 * lax.axis_index("c")
    at = jnp.stack([near, lax.axis_index("y"), lax.axis_index("zh"), way]).astype(jnp.int32)
    smem = pl.BlockSpec(memory_space=pltpu.SMEM)
    vmem = pl.BlockSpec(memory_space=pltpu.VMEM)
    ids, gates = expert_ids.T, gate_values.T
    slots = sources * cap
    share = slots // 16
    rider = 16

    def array(rows, columns=hidden):
        return jax.ShapeDtypeStruct((rows, columns), BF16)

    block = pl.pallas_call(
        pack_kernel,
        out_shape=array(tokens + 2 * top, width),
        in_specs=[pl.BlockSpec(memory_space=pltpu.HBM)] * 3,
        out_specs=vmem,
        scratch_shapes=[
            pltpu.VMEM((top, tokens), jnp.int32),
            pltpu.VMEM((top, tokens), F32),
            pltpu.SemaphoreType.DMA((3,)),
        ],
        compiler_params=pltpu.CompilerParams(vmem_limit_bytes=VMEM_LIMIT),
        cost_estimate=pl.CostEstimate(flops=0, bytes_accessed=1 << 18, transcendentals=0),
    )(grad_out, ids, gates)
    others = [lax.ppermute(block, ("b2", "b1"), [(i, i ^ rel) for i in range(4)]) for rel in (1, 2, 3)]
    picked = call(
        functools.partial(select_kernel, tokens, top, cap),
        jax.ShapeDtypeStruct((sources, cap, width), BF16),
        [smem] + [vmem] * 4,
        2 * slots * tokens * width,
        3 * slots * width,
    )(at, block, *others)
    rows = lax.all_to_all(
        picked.reshape(16, 4, cap, width), ("x", "b0", "c"), split_axis=0, concat_axis=0, tiled=True
    )
    rows = rows.reshape(4, 4, 4, cap, width).transpose(2, 0, 1, 3, 4).reshape(4, 4, share, width)
    acts = hidden_slots.reshape(4, 4, share, hidden)

    rides, *u = call(
        project_kernel,
        [array(rider), array(share)] + [array(share + rider)] * 3 + [array(3 * share)] * 4,
        [smem] + [vmem] * 3,
        2 * slots * width * hidden,
        2 * slots * (width + hidden),
    )(at, rows, w_down[0], acts)
    came = [ahead(u[r], "y", r) for r in (1, 2, 3)]
    came, u = lax.optimization_barrier((came, u))
    a, b, slot_gate = call(
        first_kernel,
        [array(share, hidden // 2)] * 2 + [jax.ShapeDtypeStruct((4, 4 * share), F32)],
        [vmem] * 5,
        4 * share * hidden,
        10 * share * hidden,
    )(u[0], rides, *came)
    a, b = ahead(a, "zh", 1), ahead(b, "zh", -1)
    came = [ahead(u[4 + r], "y", r) for r in (1, 2, 3)]

    slot_gate = slot_gate.reshape(4, 4, share).transpose(1, 0, 2).reshape(sources, cap)
    returned = lax.all_to_all(slot_gate, EXPERT, split_axis=0, concat_axis=0, tiled=True)
    gate_part = call(
        route_kernel, jax.ShapeDtypeStruct((top, tokens), F32), [vmem] * 3, 1 << 20, 1 << 16
    )(ids, gates, returned)

    one, three, own, rides = call(
        second_kernel,
        [array(share + rider)] * 2 + [array(share), array(rider)],
        [vmem] * 7,
        16 * share * hidden,
        32 * share * hidden,
    )(u[4], gate_part, *came, a, b)
    d_hidden, d_gate = call(
        finish_kernel,
        [array(share), jax.ShapeDtypeStruct((top, tokens), F32)],
        [vmem] * 5,
        4 * share * hidden,
        8 * share * hidden,
    )(own, ahead(one, "zh", 1), ahead(three, "zh", -1), rides, ahead(rides, "zh", 2))
    d_wdown = call(
        weights_kernel,
        array(width),
        [vmem] * 2,
        2 * slots * width * hidden,
        2 * slots * (width + hidden),
    )(rows, acts)
    return d_hidden.reshape(1, 4, cap, hidden), d_gate.T, d_wdown[None]


def solution(mesh):
    fine = Mesh(mesh.devices.reshape(4, 4, 4, 2, 2, 2, 2), ("zh", "y") + EXPERT)
    dp = ("zh", "y")
    return jax.shard_map(
        on_device,
        mesh=fine,
        in_specs=(
            P(EXPERT, dp),
            P(EXPERT, None),
            P(EXPERT, None),
            P(EXPERT, dp, None),
            P(EXPERT, None, None, None),
        ),
        out_specs=(P(EXPERT, dp, None, None), P(EXPERT, None), P(EXPERT, dp, None)),
        check_vma=False,
    )
```

```python
import functools

import jax
import jax.numpy as jnp
from jax import lax
from jax.experimental import pallas as pl
from jax.experimental.pallas import tpu as pltpu
from jax.sharding import Mesh
from jax.sharding import PartitionSpec as P

BF16 = jnp.bfloat16
F32 = jnp.float32
EXPERT = ("x", "b2", "b1", "b0", "c")
VMEM_LIMIT = 16 * 1024 * 1024


def call(kernel, outs, in_specs, flops, moved):
    return pl.pallas_call(
        kernel,
        out_shape=outs,
        in_specs=in_specs,
        out_specs=jax.tree.map(lambda _: pl.BlockSpec(memory_space=pltpu.VMEM), outs),
        compiler_params=pltpu.CompilerParams(vmem_limit_bytes=VMEM_LIMIT),
        cost_estimate=pl.CostEstimate(flops=flops, bytes_accessed=moved, transcendentals=0),
    )


def iota(shape, dim):
    return lax.broadcasted_iota(jnp.int32, shape, dim)


def places(ids, experts):
    tokens = ids.shape[1]
    named = jnp.zeros((experts.shape[0], tokens), F32)
    for k in range(ids.shape[0]):
        named = jnp.where(ids[k : k + 1, :] == experts, 1.0, named)
    earlier = (iota((tokens, tokens), 0) < iota((tokens, tokens), 1)).astype(F32)
    before = jnp.dot(named.astype(BF16), earlier.astype(BF16), preferred_element_type=F32)
    return jnp.where(named > 0.0, before.astype(jnp.int32), -1)


def group(near, shape):
    d = iota(shape, 0)
    return (d // 4) * 16 + near * 4 + d % 4


def pack_kernel(grad_hbm, ids_hbm, gates_hbm, out_ref, ids_ref, gates_ref, sems):
    tokens = grad_hbm.shape[0]
    copies = [
        pltpu.make_async_copy(ids_hbm, ids_ref, sems.at[0]),
        pltpu.make_async_copy(gates_hbm, gates_ref, sems.at[1]),
        pltpu.make_async_copy(grad_hbm, out_ref.at[pl.ds(0, tokens)], sems.at[2]),
    ]
    for copy in copies:
        copy.start()
    copies[0].wait()
    copies[1].wait()
    ids = ids_ref[...].astype(F32)
    gates = gates_ref[...]
    high = gates.astype(BF16).astype(F32)
    left = jnp.concatenate([ids, ids], axis=0)
    right = jnp.concatenate([high, gates - high], axis=0)
    out_ref[tokens:, :] = jnp.concatenate([left, right], axis=1).astype(BF16)
    copies[2].wait()


def select_kernel(tokens, top, cap, at_ref, *refs):
    blocks, out_ref = refs[:-1], refs[-1]
    near = at_ref[0]
    dests = out_ref.shape[0] // len(blocks)
    experts = group(near, (dests, tokens))
    slot = iota((cap, tokens), 0)
    for rel, block in enumerate(blocks):
        below = block[tokens : tokens + 2 * top, :].astype(F32)
        ids = below[:top, :tokens].astype(jnp.int32)
        gates = below[:top, tokens : 2 * tokens] + below[top:, tokens : 2 * tokens]
        place = places(ids, experts)
        weight = jnp.zeros((dests, tokens), F32)
        for k in range(top):
            weight = jnp.where(ids[k : k + 1, :] == experts, gates[k : k + 1, :], weight)
        picks, scales = [], []
        for i in range(dests):
            hit = place[i : i + 1, :] == slot
            picks.append(jnp.where(hit, 1.0, 0.0))
            scales.append(jnp.sum(jnp.where(hit, weight[i : i + 1, :], 0.0), axis=1, keepdims=True))
        picks = jnp.concatenate(picks, axis=0).astype(BF16)
        picked = jnp.dot(picks, block[:tokens, :], preferred_element_type=F32)
        index = jnp.bitwise_xor(near, rel)
        for i in range(dests):
            rows = picked[i * cap : (i + 1) * cap, :] * scales[i]
            out_ref[i * len(blocks) + index] = rows.astype(BF16)


def riding(part):
    high = part.astype(BF16).astype(F32)
    rider = jnp.concatenate([high, part - high], axis=1)
    return jnp.concatenate([rider, jnp.zeros((12, rider.shape[1]), F32)], axis=0).astype(BF16)


def ridden(rider):
    part = rider[:4].astype(F32)
    half = part.shape[1] // 2
    return part[:, :half] + part[:, half:]


def riding_gates(part):
    high = part.astype(BF16).astype(F32)
    rider = jnp.concatenate([high, part - high, jnp.zeros_like(part)], axis=1)
    return jnp.concatenate([rider, jnp.zeros_like(rider)], axis=0).astype(BF16)


def ridden_gates(rider):
    part = rider[:8, :256].astype(F32)
    return part[:, :128] + part[:, 128:]


def project_kernel(at_ref, rows_ref, w_ref, acts_ref, rider_ref, *refs):
    outs, u_ref = refs[:-1], refs[-1]
    y, zh, way = at_ref[1], at_ref[2], at_ref[3]
    w = w_ref[...]
    half = w.shape[1] // 2
    ones = jnp.ones((8, 128), F32)
    share = rows_ref.shape[2]
    pieces = rows_ref.shape[0]
    row = iota((pieces, 4 * share), 0)
    gates = jnp.zeros((pieces, 4 * share), F32)
    for r in range(pieces):
        mine = (y + way * r) % pieces
        piece = rows_ref[mine].reshape(4 * share, -1)
        u = jnp.dot(piece, w, preferred_element_type=F32)
        u_ref[...] = u.astype(BF16)
        product = u * acts_ref[:, mine].reshape(4 * share, -1).astype(F32)
        product = sum(product[:, k : k + 128] for k in range(0, w.shape[1], 128))
        line = lax.dot_general(
            ones,
            product,
            (((1,), (1,)), ((), ())),
            precision=lax.Precision.HIGHEST,
            preferred_element_type=F32,
        )
        gates = jnp.where(row == mine, line[0:1, :], gates)

        def part(far):
            x = (zh + way * far + 4) % 4
            return u_ref[pl.ds(pl.multiple_of(x * share, share), share), :]

        early, late = outs[r], outs[4 + r]
        early[:share, :] = part(2)
        value = part(3)
        early[share : 2 * share, :half] = value[:, :half]
        late[:share, half:] = value[:, half:]
        value = part(1)
        early[share : 2 * share, half:] = value[:, half:]
        late[:share, :half] = value[:, :half]
        late[share:, :] = part(0)
    rider = riding(gates)
    rider_ref[...] = rider
    for r in range(1, pieces):
        outs[r][2 * share :, :] = rider


def first_kernel(own_ref, rider_ref, one_ref, two_ref, three_ref, ahead_ref, behind_ref, gate_ref):
    share, half = ahead_ref.shape[0] // 2, ahead_ref.shape[1]
    gates = ridden(rider_ref[...])
    u = own_ref[...].astype(F32)
    for ref in (one_ref, two_ref, three_ref):
        u = u + ref[: 2 * share, :].astype(F32)
        gates = gates + ridden(ref[2 * share :, :])
    u = u.astype(BF16)
    ahead_ref[:share, :] = u[:share, :half]
    ahead_ref[share:, :] = u[share:, half:]
    behind_ref[:share, :] = u[:share, half:]
    behind_ref[share:, :] = u[share:, :half]
    gate_ref[...] = gates


def second_kernel(own_ref, gate_ref, one_ref, two_ref, three_ref, a_ref, b_ref, *outs):
    share, half = a_ref.shape[0] // 2, a_ref.shape[1]
    ahead_ref, behind_ref, mine_ref, rider_ref = outs
    u = own_ref[...].astype(F32)
    for ref in (one_ref, two_ref, three_ref):
        u = u + ref[...].astype(F32)
    rider = riding_gates(gate_ref[...])
    ahead_ref[:share, :] = (u[:share, :half] + a_ref[:share, :].astype(F32)).astype(BF16)
    behind_ref[:share, :] = (u[:share, half:] + b_ref[:share, :].astype(F32)).astype(BF16)
    ahead_ref[share:, :] = rider
    behind_ref[share:, :] = rider
    mine_ref[:, :half] = u[share:, :half] + b_ref[share:, :].astype(F32)
    mine_ref[:, half:] = u[share:, half:] + a_ref[share:, :].astype(F32)
    rider_ref[...] = rider


def finish_kernel(own_ref, one_ref, three_ref, rider_ref, two_ref, out_ref, gate_ref):
    rows, half = own_ref.shape[0], one_ref.shape[1]
    out_ref[:, :half] = (own_ref[:, :half] + one_ref[:rows, :].astype(F32)).astype(BF16)
    out_ref[:, half:] = (own_ref[:, half:] + three_ref[:rows, :].astype(F32)).astype(BF16)
    gates = ridden_gates(rider_ref[...]) + ridden_gates(two_ref[...])
    for ref in (one_ref, three_ref):
        gates = gates + ridden_gates(ref[rows:, :])
    gate_ref[...] = gates


def weights_kernel(rows_ref, acts_ref, out_ref):
    total = jnp.zeros(out_ref.shape, F32)
    for y in range(rows_ref.shape[0]):
        piece = rows_ref[y].reshape(-1, rows_ref.shape[3])
        acts = acts_ref[:, y].reshape(piece.shape[0], -1)
        total = total + lax.dot_general(
            piece, acts, (((0,), (0,)), ((), ())), preferred_element_type=F32
        )
    out_ref[...] = total.astype(BF16)


def route_kernel(ids_ref, gates_ref, returned_ref, out_ref):
    ids, gates = ids_ref[...], gates_ref[...]
    experts, cap = returned_ref.shape
    tokens = ids.shape[1]
    e = iota((experts, tokens), 0)
    place = places(ids, e)
    returned = returned_ref[...]
    found = jnp.zeros((experts, tokens), F32)
    for p in range(cap):
        found = jnp.where(place == p, returned[:, p : p + 1], found)
    lines = []
    for k in range(ids.shape[0]):
        mine = jnp.where(ids[k : k + 1, :] == e, found, 0.0)
        lines.append(jnp.sum(mine, axis=0, keepdims=True))
    out_ref[...] = jnp.concatenate(lines, axis=0) / gates


def ahead(value, axis, by):
    pairs = [(i * 2 + c, (i + (1 - 2 * c) * by) % 4 * 2 + c) for i in range(4) for c in range(2)]
    return lax.ppermute(value, (axis, "c"), pairs)


def on_device(grad_out, expert_ids, gate_values, w_down, hidden_slots):
    tokens, width = grad_out.shape
    top = expert_ids.shape[1]
    _, sources, cap, hidden = hidden_slots.shape
    near = lax.axis_index("b2") * 2 + lax.axis_index("b1")
    way = 1 - 2 * lax.axis_index("c")
    at = jnp.stack([near, lax.axis_index("y"), lax.axis_index("zh"), way]).astype(jnp.int32)
    smem = pl.BlockSpec(memory_space=pltpu.SMEM)
    vmem = pl.BlockSpec(memory_space=pltpu.VMEM)
    ids, gates = expert_ids.T, gate_values.T
    slots = sources * cap
    share = slots // 16
    rider = 16

    def array(rows, columns=hidden):
        return jax.ShapeDtypeStruct((rows, columns), BF16)

    block = pl.pallas_call(
        pack_kernel,
        out_shape=array(tokens + 2 * top, width),
        in_specs=[pl.BlockSpec(memory_space=pltpu.HBM)] * 3,
        out_specs=vmem,
        scratch_shapes=[
            pltpu.VMEM((top, tokens), jnp.int32),
            pltpu.VMEM((top, tokens), F32),
            pltpu.SemaphoreType.DMA((3,)),
        ],
        compiler_params=pltpu.CompilerParams(vmem_limit_bytes=VMEM_LIMIT),
        cost_estimate=pl.CostEstimate(flops=0, bytes_accessed=1 << 18, transcendentals=0),
    )(grad_out, ids, gates)
    others = [lax.ppermute(block, ("b2", "b1"), [(i, i ^ rel) for i in range(4)]) for rel in (1, 2, 3)]
    picked = call(
        functools.partial(select_kernel, tokens, top, cap),
        jax.ShapeDtypeStruct((sources, cap, width), BF16),
        [smem] + [vmem] * 4,
        2 * slots * tokens * width,
        3 * slots * width,
    )(at, block, *others)
    rows = lax.all_to_all(
        picked.reshape(16, 4, cap, width), ("x", "b0", "c"), split_axis=0, concat_axis=0, tiled=True
    )
    rows = rows.reshape(4, 4, 4, cap, width).transpose(2, 0, 1, 3, 4).reshape(4, 4, share, width)
    acts = hidden_slots.reshape(4, 4, share, hidden)

    half = hidden // 2
    rides, *u = pl.pallas_call(
        project_kernel,
        out_shape=[array(rider), array(2 * share)]
        + [array(2 * share + rider)] * 3
        + [array(2 * share)] * 4,
        in_specs=[smem] + [vmem] * 3,
        out_specs=[vmem] * 9,
        scratch_shapes=[pltpu.VMEM((4 * share, hidden), BF16)],
        compiler_params=pltpu.CompilerParams(vmem_limit_bytes=VMEM_LIMIT),
        cost_estimate=pl.CostEstimate(
            flops=2 * slots * width * hidden,
            bytes_accessed=2 * slots * (width + hidden),
            transcendentals=0,
        ),
    )(at, rows, w_down[0], acts)
    came = [ahead(u[r], "y", r) for r in (1, 2, 3)]
    came, u = lax.optimization_barrier((came, u))
    a, b, slot_gate = call(
        first_kernel,
        [array(2 * share, half)] * 2 + [jax.ShapeDtypeStruct((4, 4 * share), F32)],
        [vmem] * 5,
        8 * share * hidden,
        20 * share * hidden,
    )(u[0], rides, *came)
    a, b, slot_gate, u = lax.optimization_barrier((a, b, slot_gate, u))
    a, b = ahead(a, "zh", 1), ahead(b, "zh", -1)
    came = [ahead(u[4 + r], "y", r) for r in (1, 2, 3)]

    slot_gate = slot_gate.reshape(4, 4, share).transpose(1, 0, 2).reshape(sources, cap)
    returned = lax.all_to_all(slot_gate, EXPERT, split_axis=0, concat_axis=0, tiled=True)
    gate_part = call(
        route_kernel, jax.ShapeDtypeStruct((top, tokens), F32), [vmem] * 3, 1 << 20, 1 << 16
    )(ids, gates, returned)

    one, three, own, rides = call(
        second_kernel,
        [array(share + rider, half)] * 2
        + [jax.ShapeDtypeStruct((share, hidden), F32), array(rider, half)],
        [vmem] * 7,
        16 * share * hidden,
        32 * share * hidden,
    )(u[4], gate_part, *came, a, b)
    d_hidden, d_gate = call(
        finish_kernel,
        [array(share), jax.ShapeDtypeStruct((top, tokens), F32)],
        [vmem] * 5,
        4 * share * hidden,
        8 * share * hidden,
    )(own, ahead(one, "zh", 1), ahead(three, "zh", -1), rides, ahead(rides, "zh", 2))
    d_wdown = call(
        weights_kernel,
        array(width),
        [vmem] * 2,
        2 * slots * width * hidden,
        2 * slots * (width + hidden),
    )(rows, acts)
    return d_hidden.reshape(1, 4, cap, hidden), d_gate.T, d_wdown[None]


def solution(mesh):
    fine = Mesh(mesh.devices.reshape(4, 4, 4, 2, 2, 2, 2), ("zh", "y") + EXPERT)
    dp = ("zh", "y")
    return jax.shard_map(
        on_device,
        mesh=fine,
        in_specs=(
            P(EXPERT, dp),
            P(EXPERT, None),
            P(EXPERT, None),
            P(EXPERT, dp, None),
            P(EXPERT, None, None, None),
        ),
        out_specs=(P(EXPERT, dp, None, None), P(EXPERT, None), P(EXPERT, dp, None)),
        check_vma=False,
    )
```

```python
import functools

import jax
import jax.numpy as jnp
from jax import lax
from jax.experimental import pallas as pl
from jax.experimental.pallas import tpu as pltpu
from jax.sharding import Mesh
from jax.sharding import PartitionSpec as P

BF16 = jnp.bfloat16
F32 = jnp.float32
EXPERT = ("x", "b2", "b1", "b0", "c")
VMEM_LIMIT = 16 * 1024 * 1024


def call(kernel, outs, in_specs, flops, moved):
    return pl.pallas_call(
        kernel,
        out_shape=outs,
        in_specs=in_specs,
        out_specs=jax.tree.map(lambda _: pl.BlockSpec(memory_space=pltpu.VMEM), outs),
        compiler_params=pltpu.CompilerParams(vmem_limit_bytes=VMEM_LIMIT),
        cost_estimate=pl.CostEstimate(flops=flops, bytes_accessed=moved, transcendentals=0),
    )


def iota(shape, dim):
    return lax.broadcasted_iota(jnp.int32, shape, dim)


def places(ids, experts):
    tokens = ids.shape[1]
    named = jnp.zeros((experts.shape[0], tokens), F32)
    for k in range(ids.shape[0]):
        named = jnp.where(ids[k : k + 1, :] == experts, 1.0, named)
    earlier = (iota((tokens, tokens), 0) < iota((tokens, tokens), 1)).astype(F32)
    before = jnp.dot(named.astype(BF16), earlier.astype(BF16), preferred_element_type=F32)
    return jnp.where(named > 0.0, before.astype(jnp.int32), -1)


def group(near, shape):
    d = iota(shape, 0)
    return (d // 4) * 16 + near * 4 + d % 4


def pack_kernel(grad_hbm, ids_hbm, gates_hbm, out_ref, ids_ref, gates_ref, sems):
    tokens = grad_hbm.shape[0]
    copies = [
        pltpu.make_async_copy(ids_hbm, ids_ref, sems.at[0]),
        pltpu.make_async_copy(gates_hbm, gates_ref, sems.at[1]),
        pltpu.make_async_copy(grad_hbm, out_ref.at[pl.ds(0, tokens)], sems.at[2]),
    ]
    for copy in copies:
        copy.start()
    copies[0].wait()
    copies[1].wait()
    ids = ids_ref[...].astype(F32)
    gates = gates_ref[...]
    high = gates.astype(BF16).astype(F32)
    left = jnp.concatenate([ids, ids], axis=0)
    right = jnp.concatenate([high, gates - high], axis=0)
    out_ref[tokens:, :] = jnp.concatenate([left, right], axis=1).astype(BF16)
    copies[2].wait()


def select_kernel(tokens, top, cap, at_ref, *refs):
    blocks, out_ref = refs[:-1], refs[-1]
    near = at_ref[0]
    dests = out_ref.shape[0] // len(blocks)
    experts = group(near, (dests, tokens))
    slot = iota((cap, tokens), 0)
    for rel, block in enumerate(blocks):
        below = block[tokens : tokens + 2 * top, :].astype(F32)
        ids = below[:top, :tokens].astype(jnp.int32)
        gates = below[:top, tokens : 2 * tokens] + below[top:, tokens : 2 * tokens]
        place = places(ids, experts)
        weight = jnp.zeros((dests, tokens), F32)
        for k in range(top):
            weight = jnp.where(ids[k : k + 1, :] == experts, gates[k : k + 1, :], weight)
        picks, scales = [], []
        for i in range(dests):
            hit = place[i : i + 1, :] == slot
            picks.append(jnp.where(hit, 1.0, 0.0))
            scales.append(jnp.sum(jnp.where(hit, weight[i : i + 1, :], 0.0), axis=1, keepdims=True))
        picks = jnp.concatenate(picks, axis=0).astype(BF16)
        picked = jnp.dot(picks, block[:tokens, :], preferred_element_type=F32)
        index = jnp.bitwise_xor(near, rel)
        for i in range(dests):
            rows = picked[i * cap : (i + 1) * cap, :] * scales[i]
            out_ref[i * len(blocks) + index] = rows.astype(BF16)


def riding(part):
    high = part.astype(BF16).astype(F32)
    rider = jnp.concatenate([high, part - high], axis=1)
    return jnp.concatenate([rider, jnp.zeros((12, rider.shape[1]), F32)], axis=0).astype(BF16)


def ridden(rider):
    part = rider[:4].astype(F32)
    half = part.shape[1] // 2
    return part[:, :half] + part[:, half:]


def riding_gates(part):
    high = part.astype(BF16).astype(F32)
    rider = jnp.concatenate([high, part - high, jnp.zeros_like(part)], axis=1)
    return jnp.concatenate([rider, jnp.zeros_like(rider)], axis=0).astype(BF16)


def ridden_gates(rider):
    part = rider[:8, :256].astype(F32)
    return part[:, :128] + part[:, 128:]


def project_kernel(at_ref, rows_ref, w_ref, acts_ref, rider_ref, *refs):
    outs, u_ref = refs[:-1], refs[-1]
    y, zh, way = at_ref[1], at_ref[2], at_ref[3]
    w = w_ref[...]
    half = w.shape[1] // 2
    ones = jnp.ones((8, 128), F32)
    share = rows_ref.shape[2]
    pieces = rows_ref.shape[0]
    row = iota((pieces, 4 * share), 0)
    gates = jnp.zeros((pieces, 4 * share), F32)
    for r in range(pieces):
        mine = (y + way * r) % pieces
        piece = rows_ref[mine].reshape(4 * share, -1)
        u = jnp.dot(piece, w, preferred_element_type=F32)
        u_ref[...] = u.astype(BF16)
        product = u * acts_ref[:, mine].reshape(4 * share, -1).astype(F32)
        product = sum(product[:, k : k + 128] for k in range(0, w.shape[1], 128))
        line = lax.dot_general(
            ones,
            product,
            (((1,), (1,)), ((), ())),
            precision=lax.Precision.HIGHEST,
            preferred_element_type=F32,
        )
        gates = jnp.where(row == mine, line[0:1, :], gates)

        def part(far):
            x = (zh + way * far + 4) % 4
            return u_ref[pl.ds(pl.multiple_of(x * share, share), share), :]

        early, late = outs[r], outs[4 + r]
        early[:share, :] = part(2)
        value = part(3)
        early[share : 2 * share, :half] = value[:, :half]
        late[:share, half:] = value[:, half:]
        value = part(1)
        early[share : 2 * share, half:] = value[:, half:]
        late[:share, :half] = value[:, :half]
        late[share:, :] = part(0)
    rider = riding(gates)
    rider_ref[...] = rider
    for r in range(1, pieces):
        outs[r][2 * share :, :] = rider


def first_kernel(own_ref, rider_ref, one_ref, two_ref, three_ref, ahead_ref, behind_ref, gate_ref):
    share, half = ahead_ref.shape[0] // 2, ahead_ref.shape[1]
    gates = ridden(rider_ref[...])
    u = own_ref[...].astype(F32)
    for ref in (one_ref, two_ref, three_ref):
        u = u + ref[: 2 * share, :].astype(F32)
        gates = gates + ridden(ref[2 * share :, :])
    u = u.astype(BF16)
    ahead_ref[:share, :] = u[:share, :half]
    ahead_ref[share:, :] = u[share:, half:]
    behind_ref[:share, :] = u[:share, half:]
    behind_ref[share:, :] = u[share:, :half]
    gate_ref[...] = gates


def second_kernel(own_ref, gate_ref, one_ref, two_ref, three_ref, a_ref, b_ref, *outs):
    share, half = a_ref.shape[0] // 2, a_ref.shape[1]
    ahead_ref, behind_ref, mine_ref = outs
    u = own_ref[...].astype(F32)
    for ref in (one_ref, two_ref, three_ref):
        u = u + ref[...].astype(F32)
    ahead_ref[:share, :] = (u[:share, :half] + a_ref[:share, :].astype(F32)).astype(BF16)
    behind_ref[:share, :] = (u[:share, half:] + b_ref[:share, :].astype(F32)).astype(BF16)
    ahead_ref[share:, :] = riding_gates(gate_ref[...])
    mine_ref[:, :half] = u[share:, :half] + b_ref[share:, :].astype(F32)
    mine_ref[:, half:] = u[share:, half:] + a_ref[share:, :].astype(F32)


def finish_kernel(own_ref, one_ref, three_ref, part_ref, out_ref, gate_ref):
    rows, half = own_ref.shape[0], one_ref.shape[1]
    out_ref[:, :half] = (own_ref[:, :half] + one_ref[:rows, :].astype(F32)).astype(BF16)
    out_ref[:, half:] = (own_ref[:, half:] + three_ref[:rows, :].astype(F32)).astype(BF16)
    gate_ref[...] = part_ref[...] + ridden_gates(one_ref[rows:, :])


def weights_kernel(rows_ref, acts_ref, out_ref):
    total = jnp.zeros(out_ref.shape, F32)
    for y in range(rows_ref.shape[0]):
        piece = rows_ref[y].reshape(-1, rows_ref.shape[3])
        acts = acts_ref[:, y].reshape(piece.shape[0], -1)
        total = total + lax.dot_general(
            piece, acts, (((0,), (0,)), ((), ())), preferred_element_type=F32
        )
    out_ref[...] = total.astype(BF16)


def route_kernel(ids_ref, gates_ref, returned_ref, out_ref):
    ids, gates = ids_ref[...], gates_ref[...]
    experts, cap = returned_ref.shape
    tokens = ids.shape[1]
    e = iota((experts, tokens), 0)
    place = places(ids, e)
    returned = returned_ref[...]
    found = jnp.zeros((experts, tokens), F32)
    for p in range(cap):
        found = jnp.where(place == p, returned[:, p : p + 1], found)
    lines = []
    for k in range(ids.shape[0]):
        mine = jnp.where(ids[k : k + 1, :] == e, found, 0.0)
        lines.append(jnp.sum(mine, axis=0, keepdims=True))
    out_ref[...] = jnp.concatenate(lines, axis=0) / gates


def ahead(value, axis, by):
    pairs = [(i * 2 + c, (i + (1 - 2 * c) * by) % 4 * 2 + c) for i in range(4) for c in range(2)]
    return lax.ppermute(value, (axis, "c"), pairs)


def on_device(grad_out, expert_ids, gate_values, w_down, hidden_slots):
    tokens, width = grad_out.shape
    top = expert_ids.shape[1]
    _, sources, cap, hidden = hidden_slots.shape
    near = lax.axis_index("b2") * 2 + lax.axis_index("b1")
    way = 1 - 2 * lax.axis_index("c")
    at = jnp.stack([near, lax.axis_index("y"), lax.axis_index("zh"), way]).astype(jnp.int32)
    smem = pl.BlockSpec(memory_space=pltpu.SMEM)
    vmem = pl.BlockSpec(memory_space=pltpu.VMEM)
    ids, gates = expert_ids.T, gate_values.T
    slots = sources * cap
    share = slots // 16
    rider = 16

    def array(rows, columns=hidden):
        return jax.ShapeDtypeStruct((rows, columns), BF16)

    block = pl.pallas_call(
        pack_kernel,
        out_shape=array(tokens + 2 * top, width),
        in_specs=[pl.BlockSpec(memory_space=pltpu.HBM)] * 3,
        out_specs=vmem,
        scratch_shapes=[
            pltpu.VMEM((top, tokens), jnp.int32),
            pltpu.VMEM((top, tokens), F32),
            pltpu.SemaphoreType.DMA((3,)),
        ],
        compiler_params=pltpu.CompilerParams(vmem_limit_bytes=VMEM_LIMIT),
        cost_estimate=pl.CostEstimate(flops=0, bytes_accessed=1 << 18, transcendentals=0),
    )(grad_out, ids, gates)
    others = [lax.ppermute(block, ("b2", "b1"), [(i, i ^ rel) for i in range(4)]) for rel in (1, 2, 3)]
    picked = call(
        functools.partial(select_kernel, tokens, top, cap),
        jax.ShapeDtypeStruct((sources, cap, width), BF16),
        [smem] + [vmem] * 4,
        2 * slots * tokens * width,
        3 * slots * width,
    )(at, block, *others)
    rows = lax.all_to_all(
        picked.reshape(16, 4, cap, width), ("x", "b0", "c"), split_axis=0, concat_axis=0, tiled=True
    )
    rows = rows.reshape(4, 4, 4, cap, width).transpose(2, 0, 1, 3, 4).reshape(4, 4, share, width)
    acts = hidden_slots.reshape(4, 4, share, hidden)

    half = hidden // 2
    rides, *u = pl.pallas_call(
        project_kernel,
        out_shape=[array(rider), array(2 * share)]
        + [array(2 * share + rider)] * 3
        + [array(2 * share)] * 4,
        in_specs=[smem] + [vmem] * 3,
        out_specs=[vmem] * 9,
        scratch_shapes=[pltpu.VMEM((4 * share, hidden), BF16)],
        compiler_params=pltpu.CompilerParams(vmem_limit_bytes=VMEM_LIMIT),
        cost_estimate=pl.CostEstimate(
            flops=2 * slots * width * hidden,
            bytes_accessed=2 * slots * (width + hidden),
            transcendentals=0,
        ),
    )(at, rows, w_down[0], acts)
    came = [ahead(u[r], "y", r) for r in (1, 2, 3)]
    came, u = lax.optimization_barrier((came, u))
    a, b, slot_gate = call(
        first_kernel,
        [array(2 * share, half)] * 2 + [jax.ShapeDtypeStruct((4, 4 * share), F32)],
        [vmem] * 5,
        8 * share * hidden,
        20 * share * hidden,
    )(u[0], rides, *came)
    a, b, slot_gate, u = lax.optimization_barrier((a, b, slot_gate, u))
    opposite = ahead(slot_gate, "zh", 2)
    a, b = ahead(a, "zh", 1), ahead(b, "zh", -1)
    came = [ahead(u[4 + r], "y", r) for r in (1, 2, 3)]

    slot_gate = slot_gate + opposite
    slot_gate = slot_gate.reshape(4, 4, share).transpose(1, 0, 2).reshape(sources, cap)
    returned = lax.all_to_all(slot_gate, EXPERT, split_axis=0, concat_axis=0, tiled=True)
    gate_part = call(
        route_kernel, jax.ShapeDtypeStruct((top, tokens), F32), [vmem] * 3, 1 << 20, 1 << 16
    )(ids, gates, returned)

    one, three, own = call(
        second_kernel,
        [
            array(share + rider, half),
            array(share, half),
            jax.ShapeDtypeStruct((share, hidden), F32),
        ],
        [vmem] * 7,
        16 * share * hidden,
        32 * share * hidden,
    )(u[4], gate_part, *came, a, b)
    d_hidden, d_gate = call(
        finish_kernel,
        [array(share), jax.ShapeDtypeStruct((top, tokens), F32)],
        [vmem] * 4,
        4 * share * hidden,
        8 * share * hidden,
    )(own, ahead(one, "zh", 1), ahead(three, "zh", -1), gate_part)
    d_wdown = call(
        weights_kernel,
        array(width),
        [vmem] * 2,
        2 * slots * width * hidden,
        2 * slots * (width + hidden),
    )(rows, acts)
    return d_hidden.reshape(1, 4, cap, hidden), d_gate.T, d_wdown[None]


def solution(mesh):
    fine = Mesh(mesh.devices.reshape(4, 4, 4, 2, 2, 2, 2), ("zh", "y") + EXPERT)
    dp = ("zh", "y")
    return jax.shard_map(
        on_device,
        mesh=fine,
        in_specs=(
            P(EXPERT, dp),
            P(EXPERT, None),
            P(EXPERT, None),
            P(EXPERT, dp, None),
            P(EXPERT, None, None, None),
        ),
        out_specs=(P(EXPERT, dp, None, None), P(EXPERT, None), P(EXPERT, dp, None)),
        check_vma=False,
    )
```

```python
import functools

import jax
import jax.numpy as jnp
from jax import lax
from jax.experimental import pallas as pl
from jax.experimental.pallas import tpu as pltpu
from jax.sharding import Mesh
from jax.sharding import PartitionSpec as P

BF16 = jnp.bfloat16
F32 = jnp.float32
EXPERT = ("x", "b2", "b1", "b0", "c")
VMEM_LIMIT = 16 * 1024 * 1024


def call(kernel, outs, in_specs, flops, moved):
    return pl.pallas_call(
        kernel,
        out_shape=outs,
        in_specs=in_specs,
        out_specs=jax.tree.map(lambda _: pl.BlockSpec(memory_space=pltpu.VMEM), outs),
        compiler_params=pltpu.CompilerParams(vmem_limit_bytes=VMEM_LIMIT),
        cost_estimate=pl.CostEstimate(flops=flops, bytes_accessed=moved, transcendentals=0),
    )


def iota(shape, dim):
    return lax.broadcasted_iota(jnp.int32, shape, dim)


def places(ids, experts):
    tokens = ids.shape[1]
    named = jnp.zeros((experts.shape[0], tokens), F32)
    for k in range(ids.shape[0]):
        named = jnp.where(ids[k : k + 1, :] == experts, 1.0, named)
    earlier = (iota((tokens, tokens), 0) < iota((tokens, tokens), 1)).astype(F32)
    before = jnp.dot(named.astype(BF16), earlier.astype(BF16), preferred_element_type=F32)
    return jnp.where(named > 0.0, before.astype(jnp.int32), -1)


def group(near, shape):
    d = iota(shape, 0)
    return (d // 4) * 16 + near * 4 + d % 4


def pack_kernel(grad_hbm, ids_hbm, gates_hbm, out_ref, ids_ref, gates_ref, sems):
    tokens = grad_hbm.shape[0]
    copies = [
        pltpu.make_async_copy(ids_hbm, ids_ref, sems.at[0]),
        pltpu.make_async_copy(gates_hbm, gates_ref, sems.at[1]),
        pltpu.make_async_copy(grad_hbm, out_ref.at[pl.ds(0, tokens)], sems.at[2]),
    ]
    for copy in copies:
        copy.start()
    copies[0].wait()
    copies[1].wait()
    ids = ids_ref[...].astype(F32)
    gates = gates_ref[...]
    high = gates.astype(BF16).astype(F32)
    left = jnp.concatenate([ids, ids], axis=0)
    right = jnp.concatenate([high, gates - high], axis=0)
    out_ref[tokens:, :] = jnp.concatenate([left, right], axis=1).astype(BF16)
    copies[2].wait()


def select_kernel(tokens, top, cap, at_ref, *refs):
    blocks, out_ref = refs[:-1], refs[-1]
    near = at_ref[0]
    dests = out_ref.shape[0] // len(blocks)
    experts = group(near, (dests, tokens))
    slot = iota((cap, tokens), 0)
    for rel, block in enumerate(blocks):
        below = block[tokens : tokens + 2 * top, :].astype(F32)
        ids = below[:top, :tokens].astype(jnp.int32)
        gates = below[:top, tokens : 2 * tokens] + below[top:, tokens : 2 * tokens]
        place = places(ids, experts)
        weight = jnp.zeros((dests, tokens), F32)
        for k in range(top):
            weight = jnp.where(ids[k : k + 1, :] == experts, gates[k : k + 1, :], weight)
        picks, scales = [], []
        for i in range(dests):
            hit = place[i : i + 1, :] == slot
            picks.append(jnp.where(hit, 1.0, 0.0))
            scales.append(jnp.sum(jnp.where(hit, weight[i : i + 1, :], 0.0), axis=1, keepdims=True))
        picks = jnp.concatenate(picks, axis=0).astype(BF16)
        picked = jnp.dot(picks, block[:tokens, :], preferred_element_type=F32)
        index = jnp.bitwise_xor(near, rel)
        for i in range(dests):
            rows = picked[i * cap : (i + 1) * cap, :] * scales[i]
            out_ref[i * len(blocks) + index] = rows.astype(BF16)


def riding(part):
    high = part.astype(BF16).astype(F32)
    rider = jnp.concatenate([high, part - high], axis=1)
    return jnp.concatenate([rider, jnp.zeros((12, rider.shape[1]), F32)], axis=0).astype(BF16)


def ridden(rider):
    part = rider[:4].astype(F32)
    half = part.shape[1] // 2
    return part[:, :half] + part[:, half:]


def riding_gates(part):
    high = part.astype(BF16).astype(F32)
    rider = jnp.concatenate([high, part - high, jnp.zeros_like(part)], axis=1)
    return jnp.concatenate([rider, jnp.zeros_like(rider)], axis=0).astype(BF16)


def ridden_gates(rider):
    part = rider[:8, :256].astype(F32)
    return part[:, :128] + part[:, 128:]


def project_kernel(at_ref, rows_ref, w_ref, acts_ref, rider_ref, *refs):
    outs, u_ref = refs[:-1], refs[-1]
    y, zh, way = at_ref[1], at_ref[2], at_ref[3]
    w = w_ref[...]
    half = w.shape[1] // 2
    ones = jnp.ones((8, 128), F32)
    share = rows_ref.shape[2]
    pieces = rows_ref.shape[0]
    row = iota((pieces, 4 * share), 0)
    gates = jnp.zeros((pieces, 4 * share), F32)
    for r in range(pieces):
        mine = (y + way * r) % pieces
        piece = rows_ref[mine].reshape(4 * share, -1)
        u = jnp.dot(piece, w, preferred_element_type=F32)
        u_ref[...] = u.astype(BF16)
        product = u * acts_ref[:, mine].reshape(4 * share, -1).astype(F32)
        product = sum(product[:, k : k + 128] for k in range(0, w.shape[1], 128))
        line = lax.dot_general(
            ones,
            product,
            (((1,), (1,)), ((), ())),
            precision=lax.Precision.HIGHEST,
            preferred_element_type=F32,
        )
        gates = jnp.where(row == mine, line[0:1, :], gates)

        def part(far):
            x = (zh + way * far + 4) % 4
            return u_ref[pl.ds(pl.multiple_of(x * share, share), share), :]

        early, late = outs[r], outs[4 + r]
        early[:share, :] = part(2)
        value = part(3)
        early[share : 2 * share, :half] = value[:, :half]
        late[:share, half:] = value[:, half:]
        value = part(1)
        early[share : 2 * share, half:] = value[:, half:]
        late[:share, :half] = value[:, :half]
        late[share:, :] = part(0)
    rider = riding(gates)
    rider_ref[...] = rider
    for r in range(1, pieces):
        outs[r][2 * share :, :] = rider


def first_kernel(own_ref, rider_ref, one_ref, two_ref, three_ref, ahead_ref, behind_ref, gate_ref):
    share, half = ahead_ref.shape[0] // 2, ahead_ref.shape[1]
    gates = ridden(rider_ref[...])
    u = own_ref[...].astype(F32)
    for ref in (one_ref, two_ref, three_ref):
        u = u + ref[: 2 * share, :].astype(F32)
        gates = gates + ridden(ref[2 * share :, :])
    u = u.astype(BF16)
    ahead_ref[:share, :] = u[:share, :half]
    ahead_ref[share:, :] = u[share:, half:]
    behind_ref[:share, :] = u[:share, half:]
    behind_ref[share:, :] = u[share:, :half]
    gate_ref[...] = gates


def second_kernel(own_ref, gate_ref, one_ref, two_ref, three_ref, a_ref, b_ref, *outs):
    share, half = a_ref.shape[0] // 2, a_ref.shape[1]
    ahead_ref, behind_ref, mine_ref = outs
    u = own_ref[...].astype(F32)
    for ref in (one_ref, two_ref, three_ref):
        u = u + ref[...].astype(F32)
    ahead_ref[:share, :] = (u[:share, :half] + a_ref[:share, :].astype(F32)).astype(BF16)
    behind_ref[:share, :] = (u[:share, half:] + b_ref[:share, :].astype(F32)).astype(BF16)
    ahead_ref[share:, :] = riding_gates(gate_ref[...])
    mine_ref[:, :half] = u[share:, :half] + b_ref[share:, :].astype(F32)
    mine_ref[:, half:] = u[share:, half:] + a_ref[share:, :].astype(F32)


def finish_kernel(own_ref, one_ref, three_ref, part_ref, out_ref, gate_ref):
    rows, half = own_ref.shape[0], one_ref.shape[1]
    out_ref[:, :half] = (own_ref[:, :half] + one_ref[:rows, :].astype(F32)).astype(BF16)
    out_ref[:, half:] = (own_ref[:, half:] + three_ref[:rows, :].astype(F32)).astype(BF16)
    gate_ref[...] = part_ref[...] + ridden_gates(one_ref[rows:, :])


def weights_kernel(rows_ref, acts_ref, out_ref):
    total = jnp.zeros(out_ref.shape, F32)
    for y in range(rows_ref.shape[0]):
        piece = rows_ref[y].reshape(-1, rows_ref.shape[3])
        acts = acts_ref[:, y].reshape(piece.shape[0], -1)
        total = total + lax.dot_general(
            piece, acts, (((0,), (0,)), ((), ())), preferred_element_type=F32
        )
    out_ref[...] = total.astype(BF16)


def route_kernel(ids_ref, gates_ref, returned_ref, out_ref):
    ids, gates = ids_ref[...], gates_ref[...]
    experts, cap = returned_ref.shape
    tokens = ids.shape[1]
    e = iota((experts, tokens), 0)
    place = places(ids, e)
    returned = returned_ref[...]
    found = jnp.zeros((experts, tokens), F32)
    for p in range(cap):
        found = jnp.where(place == p, returned[:, p : p + 1], found)
    lines = []
    for k in range(ids.shape[0]):
        mine = jnp.where(ids[k : k + 1, :] == e, found, 0.0)
        lines.append(jnp.sum(mine, axis=0, keepdims=True))
    out_ref[...] = jnp.concatenate(lines, axis=0) / gates


def ahead(value, axis, by):
    pairs = [(i * 2 + c, (i + (1 - 2 * c) * by) % 4 * 2 + c) for i in range(4) for c in range(2)]
    return lax.ppermute(value, (axis, "c"), pairs)


def on_device(grad_out, expert_ids, gate_values, w_down, hidden_slots):
    tokens, width = grad_out.shape
    top = expert_ids.shape[1]
    _, sources, cap, hidden = hidden_slots.shape
    near = lax.axis_index("b2") * 2 + lax.axis_index("b1")
    way = 1 - 2 * lax.axis_index("c")
    at = jnp.stack([near, lax.axis_index("y"), lax.axis_index("zh"), way]).astype(jnp.int32)
    smem = pl.BlockSpec(memory_space=pltpu.SMEM)
    vmem = pl.BlockSpec(memory_space=pltpu.VMEM)
    ids, gates = expert_ids.T, gate_values.T
    slots = sources * cap
    share = slots // 16
    rider = 16

    def array(rows, columns=hidden):
        return jax.ShapeDtypeStruct((rows, columns), BF16)

    block = pl.pallas_call(
        pack_kernel,
        out_shape=array(tokens + 2 * top, width),
        in_specs=[pl.BlockSpec(memory_space=pltpu.HBM)] * 3,
        out_specs=vmem,
        scratch_shapes=[
            pltpu.VMEM((top, tokens), jnp.int32),
            pltpu.VMEM((top, tokens), F32),
            pltpu.SemaphoreType.DMA((3,)),
        ],
        compiler_params=pltpu.CompilerParams(vmem_limit_bytes=VMEM_LIMIT),
        cost_estimate=pl.CostEstimate(flops=0, bytes_accessed=1 << 18, transcendentals=0),
    )(grad_out, ids, gates)
    others = [lax.ppermute(block, ("b2", "b1"), [(i, i ^ rel) for i in range(4)]) for rel in (1, 2, 3)]
    picked = call(
        functools.partial(select_kernel, tokens, top, cap),
        jax.ShapeDtypeStruct((sources, cap, width), BF16),
        [smem] + [vmem] * 4,
        2 * slots * tokens * width,
        3 * slots * width,
    )(at, block, *others)
    rows = lax.all_to_all(
        picked.reshape(16, 4, cap, width), ("x", "b0", "c"), split_axis=0, concat_axis=0, tiled=True
    )
    rows = rows.reshape(4, 4, 4, cap, width).transpose(2, 0, 1, 3, 4).reshape(4, 4, share, width)
    acts = hidden_slots.reshape(4, 4, share, hidden)

    half = hidden // 2
    rides, *u = pl.pallas_call(
        project_kernel,
        out_shape=[array(rider), array(2 * share)]
        + [array(2 * share + rider)] * 3
        + [array(2 * share)] * 4,
        in_specs=[smem] + [vmem] * 3,
        out_specs=[vmem] * 9,
        scratch_shapes=[pltpu.VMEM((4 * share, hidden), BF16)],
        compiler_params=pltpu.CompilerParams(vmem_limit_bytes=VMEM_LIMIT),
        cost_estimate=pl.CostEstimate(
            flops=2 * slots * width * hidden,
            bytes_accessed=2 * slots * (width + hidden),
            transcendentals=0,
        ),
    )(at, rows, w_down[0], acts)
    came = [ahead(u[r], "y", r) for r in (1, 2, 3)]
    came, u = lax.optimization_barrier((came, u))
    a, b, slot_gate = call(
        first_kernel,
        [array(2 * share, half)] * 2 + [jax.ShapeDtypeStruct((4, 4 * share), F32)],
        [vmem] * 5,
        8 * share * hidden,
        20 * share * hidden,
    )(u[0], rides, *came)
    a, b, slot_gate, u = lax.optimization_barrier((a, b, slot_gate, u))
    a, b = ahead(a, "zh", 1), ahead(b, "zh", -1)
    came = [ahead(u[4 + r], "y", r) for r in (1, 2, 3)]

    slot_gate = slot_gate.reshape(4, 4, share).transpose(1, 0, 2).reshape(sources, cap)
    returned = lax.all_to_all(slot_gate, EXPERT, split_axis=0, concat_axis=0, tiled=True)
    gate_part = call(
        route_kernel, jax.ShapeDtypeStruct((top, tokens), F32), [vmem] * 3, 1 << 20, 1 << 16
    )(ids, gates, returned)

    a, b, came, gate_part = lax.optimization_barrier((a, b, came, gate_part))
    gate_part = gate_part + ahead(gate_part, "zh", 2)

    one, three, own = call(
        second_kernel,
        [
            array(share + rider, half),
            array(share, half),
            jax.ShapeDtypeStruct((share, hidden), F32),
        ],
        [vmem] * 7,
        16 * share * hidden,
        32 * share * hidden,
    )(u[4], gate_part, *came, a, b)
    d_hidden, d_gate = call(
        finish_kernel,
        [array(share), jax.ShapeDtypeStruct((top, tokens), F32)],
        [vmem] * 4,
        4 * share * hidden,
        8 * share * hidden,
    )(own, ahead(one, "zh", 1), ahead(three, "zh", -1), gate_part)
    d_wdown = call(
        weights_kernel,
        array(width),
        [vmem] * 2,
        2 * slots * width * hidden,
        2 * slots * (width + hidden),
    )(rows, acts)
    return d_hidden.reshape(1, 4, cap, hidden), d_gate.T, d_wdown[None]


def solution(mesh):
    fine = Mesh(mesh.devices.reshape(4, 4, 4, 2, 2, 2, 2), ("zh", "y") + EXPERT)
    dp = ("zh", "y")
    return jax.shard_map(
        on_device,
        mesh=fine,
        in_specs=(
            P(EXPERT, dp),
            P(EXPERT, None),
            P(EXPERT, None),
            P(EXPERT, dp, None),
            P(EXPERT, None, None, None),
        ),
        out_specs=(P(EXPERT, dp, None, None), P(EXPERT, None), P(EXPERT, dp, None)),
        check_vma=False,
    )
```

```python
import functools

import jax
import jax.numpy as jnp
from jax import lax
from jax.experimental import pallas as pl
from jax.experimental.pallas import tpu as pltpu
from jax.sharding import Mesh
from jax.sharding import PartitionSpec as P

BF16 = jnp.bfloat16
F32 = jnp.float32
EXPERT = ("x", "b2", "b1", "b0", "c")
VMEM_LIMIT = 16 * 1024 * 1024


def call(kernel, outs, in_specs, flops, moved):
    return pl.pallas_call(
        kernel,
        out_shape=outs,
        in_specs=in_specs,
        out_specs=jax.tree.map(lambda _: pl.BlockSpec(memory_space=pltpu.VMEM), outs),
        compiler_params=pltpu.CompilerParams(vmem_limit_bytes=VMEM_LIMIT),
        cost_estimate=pl.CostEstimate(flops=flops, bytes_accessed=moved, transcendentals=0),
    )


def iota(shape, dim):
    return lax.broadcasted_iota(jnp.int32, shape, dim)


def places(ids, experts):
    tokens = ids.shape[1]
    named = jnp.zeros((experts.shape[0], tokens), F32)
    for k in range(ids.shape[0]):
        named = jnp.where(ids[k : k + 1, :] == experts, 1.0, named)
    earlier = (iota((tokens, tokens), 0) < iota((tokens, tokens), 1)).astype(F32)
    before = jnp.dot(named.astype(BF16), earlier.astype(BF16), preferred_element_type=F32)
    return jnp.where(named > 0.0, before.astype(jnp.int32), -1)


def group(near, shape):
    d = iota(shape, 0)
    return (d // 4) * 16 + near * 4 + d % 4


def pack_kernel(grad_hbm, ids_hbm, gates_hbm, out_ref, ids_ref, gates_ref, sems):
    tokens = grad_hbm.shape[0]
    copies = [
        pltpu.make_async_copy(ids_hbm, ids_ref, sems.at[0]),
        pltpu.make_async_copy(gates_hbm, gates_ref, sems.at[1]),
        pltpu.make_async_copy(grad_hbm, out_ref.at[pl.ds(0, tokens)], sems.at[2]),
    ]
    for copy in copies:
        copy.start()
    copies[0].wait()
    copies[1].wait()
    ids = ids_ref[...].astype(F32)
    gates = gates_ref[...]
    high = gates.astype(BF16).astype(F32)
    left = jnp.concatenate([ids, ids], axis=0)
    right = jnp.concatenate([high, gates - high], axis=0)
    out_ref[tokens:, :] = jnp.concatenate([left, right], axis=1).astype(BF16)
    copies[2].wait()


def select_kernel(tokens, top, cap, at_ref, *refs):
    blocks, out_ref = refs[:-1], refs[-1]
    near = at_ref[0]
    dests = out_ref.shape[0] // len(blocks)
    experts = group(near, (dests, tokens))
    slot = iota((cap, tokens), 0)
    for rel, block in enumerate(blocks):
        below = block[tokens : tokens + 2 * top, :].astype(F32)
        ids = below[:top, :tokens].astype(jnp.int32)
        gates = below[:top, tokens : 2 * tokens] + below[top:, tokens : 2 * tokens]
        place = places(ids, experts)
        weight = jnp.zeros((dests, tokens), F32)
        for k in range(top):
            weight = jnp.where(ids[k : k + 1, :] == experts, gates[k : k + 1, :], weight)
        picks, scales = [], []
        for i in range(dests):
            hit = place[i : i + 1, :] == slot
            picks.append(jnp.where(hit, 1.0, 0.0))
            scales.append(jnp.sum(jnp.where(hit, weight[i : i + 1, :], 0.0), axis=1, keepdims=True))
        picks = jnp.concatenate(picks, axis=0).astype(BF16)
        picked = jnp.dot(picks, block[:tokens, :], preferred_element_type=F32)
        index = jnp.bitwise_xor(near, rel)
        for i in range(dests):
            rows = picked[i * cap : (i + 1) * cap, :] * scales[i]
            out_ref[i * len(blocks) + index] = rows.astype(BF16)


def riding(part):
    high = part.astype(BF16).astype(F32)
    rider = jnp.concatenate([high, part - high], axis=1)
    return jnp.concatenate([rider, jnp.zeros((12, rider.shape[1]), F32)], axis=0).astype(BF16)


def ridden(rider):
    part = rider[:4].astype(F32)
    half = part.shape[1] // 2
    return part[:, :half] + part[:, half:]


def riding_gates(part):
    high = part.astype(BF16).astype(F32)
    rider = jnp.concatenate([high, part - high, jnp.zeros_like(part)], axis=1)
    return jnp.concatenate([rider, jnp.zeros_like(rider)], axis=0).astype(BF16)


def ridden_gates(rider):
    part = rider[:8, :256].astype(F32)
    return part[:, :128] + part[:, 128:]


def project_kernel(at_ref, rows_ref, w_ref, acts_ref, rider_ref, *refs):
    outs, u_ref = refs[:-1], refs[-1]
    y, zh, way = at_ref[1], at_ref[2], at_ref[3]
    w = w_ref[...]
    half = w.shape[1] // 2
    ones = jnp.ones((8, 128), F32)
    share = rows_ref.shape[2]
    pieces = rows_ref.shape[0]
    row = iota((pieces, 4 * share), 0)
    gates = jnp.zeros((pieces, 4 * share), F32)
    for r in range(pieces):
        mine = (y + way * r) % pieces
        piece = rows_ref[mine].reshape(4 * share, -1)
        u = jnp.dot(piece, w, preferred_element_type=F32)
        u_ref[...] = u.astype(BF16)
        product = u * acts_ref[:, mine].reshape(4 * share, -1).astype(F32)
        product = sum(product[:, k : k + 128] for k in range(0, w.shape[1], 128))
        line = lax.dot_general(
            ones,
            product,
            (((1,), (1,)), ((), ())),
            precision=lax.Precision.HIGHEST,
            preferred_element_type=F32,
        )
        gates = jnp.where(row == mine, line[0:1, :], gates)

        def part(far):
            x = (zh + way * far + 4) % 4
            return u_ref[pl.ds(pl.multiple_of(x * share, share), share), :]

        early, late = outs[r], outs[4 + r]
        early[:share, :] = part(2)
        value = part(3)
        early[share : 2 * share, :half] = value[:, :half]
        late[:share, half:] = value[:, half:]
        value = part(1)
        early[share : 2 * share, half:] = value[:, half:]
        late[:share, :half] = value[:, :half]
        late[share:, :] = part(0)
    rider = riding(gates)
    rider_ref[...] = rider
    for r in range(1, pieces):
        outs[r][2 * share :, :] = rider


def first_kernel(own_ref, rider_ref, one_ref, two_ref, three_ref, ahead_ref, behind_ref, gate_ref):
    share, half = ahead_ref.shape[0] // 2, ahead_ref.shape[1]
    gates = ridden(rider_ref[...])
    u = own_ref[...].astype(F32)
    for ref in (one_ref, two_ref, three_ref):
        u = u + ref[: 2 * share, :].astype(F32)
        gates = gates + ridden(ref[2 * share :, :])
    u = u.astype(BF16)
    ahead_ref[:share, :] = u[:share, :half]
    ahead_ref[share:, :] = u[share:, half:]
    behind_ref[:share, :] = u[:share, half:]
    behind_ref[share:, :] = u[share:, :half]
    gate_ref[...] = gates


def second_kernel(own_ref, gate_ref, one_ref, two_ref, three_ref, a_ref, b_ref, *outs):
    share, half = a_ref.shape[0] // 2, a_ref.shape[1]
    ahead_ref, behind_ref, mine_ref, rider_ref = outs
    u = own_ref[...].astype(F32)
    for ref in (one_ref, two_ref, three_ref):
        u = u + ref[...].astype(F32)
    rider = riding_gates(gate_ref[...])
    ahead_ref[:share, :] = (u[:share, :half] + a_ref[:share, :].astype(F32)).astype(BF16)
    behind_ref[:share, :] = (u[:share, half:] + b_ref[:share, :].astype(F32)).astype(BF16)
    ahead_ref[share:, :] = rider
    behind_ref[share:, :] = rider
    mine_ref[:, :half] = u[share:, :half] + b_ref[share:, :].astype(F32)
    mine_ref[:, half:] = u[share:, half:] + a_ref[share:, :].astype(F32)
    rider_ref[...] = rider


def finish_kernel(own_ref, one_ref, three_ref, rider_ref, two_ref, out_ref, gate_ref):
    rows, half = own_ref.shape[0], one_ref.shape[1]
    out_ref[:, :half] = (own_ref[:, :half] + one_ref[:rows, :].astype(F32)).astype(BF16)
    out_ref[:, half:] = (own_ref[:, half:] + three_ref[:rows, :].astype(F32)).astype(BF16)
    gates = ridden_gates(rider_ref[...]) + ridden_gates(two_ref[...])
    for ref in (one_ref, three_ref):
        gates = gates + ridden_gates(ref[rows:, :])
    gate_ref[...] = gates


def weights_kernel(rows_ref, acts_ref, out_ref):
    total = jnp.zeros(out_ref.shape, F32)
    for y in range(rows_ref.shape[0]):
        piece = rows_ref[y].reshape(-1, rows_ref.shape[3])
        acts = acts_ref[:, y].reshape(piece.shape[0], -1)
        total = total + lax.dot_general(
            piece, acts, (((0,), (0,)), ((), ())), preferred_element_type=F32
        )
    out_ref[...] = total.astype(BF16)


def route_kernel(ids_ref, gates_ref, returned_ref, out_ref):
    ids, gates = ids_ref[...], gates_ref[...]
    experts, cap = returned_ref.shape
    tokens = ids.shape[1]
    e = iota((experts, tokens), 0)
    place = places(ids, e)
    returned = returned_ref[...]
    found = jnp.zeros((experts, tokens), F32)
    for p in range(cap):
        found = jnp.where(place == p, returned[:, p : p + 1], found)
    lines = []
    for k in range(ids.shape[0]):
        mine = jnp.where(ids[k : k + 1, :] == e, found, 0.0)
        lines.append(jnp.sum(mine, axis=0, keepdims=True))
    out_ref[...] = jnp.concatenate(lines, axis=0) / gates


def ahead(value, axis, by):
    pairs = [(i * 2 + c, (i + (1 - 2 * c) * by) % 4 * 2 + c) for i in range(4) for c in range(2)]
    return lax.ppermute(value, (axis, "c"), pairs)


def on_device(grad_out, expert_ids, gate_values, w_down, hidden_slots):
    tokens, width = grad_out.shape
    top = expert_ids.shape[1]
    _, sources, cap, hidden = hidden_slots.shape
    near = lax.axis_index("b2") * 2 + lax.axis_index("b1")
    way = 1 - 2 * lax.axis_index("c")
    at = jnp.stack([near, lax.axis_index("y"), lax.axis_index("zh"), way]).astype(jnp.int32)
    smem = pl.BlockSpec(memory_space=pltpu.SMEM)
    vmem = pl.BlockSpec(memory_space=pltpu.VMEM)
    ids, gates = expert_ids.T, gate_values.T
    slots = sources * cap
    share = slots // 16
    rider = 16

    def array(rows, columns=hidden):
        return jax.ShapeDtypeStruct((rows, columns), BF16)

    block = pl.pallas_call(
        pack_kernel,
        out_shape=array(tokens + 2 * top, width),
        in_specs=[pl.BlockSpec(memory_space=pltpu.HBM)] * 3,
        out_specs=vmem,
        scratch_shapes=[
            pltpu.VMEM((top, tokens), jnp.int32),
            pltpu.VMEM((top, tokens), F32),
            pltpu.SemaphoreType.DMA((3,)),
        ],
        compiler_params=pltpu.CompilerParams(vmem_limit_bytes=VMEM_LIMIT),
        cost_estimate=pl.CostEstimate(flops=0, bytes_accessed=1 << 18, transcendentals=0),
    )(grad_out, ids, gates)
    others = [lax.ppermute(block, ("b2", "b1"), [(i, i ^ rel) for i in range(4)]) for rel in (1, 2, 3)]
    picked = call(
        functools.partial(select_kernel, tokens, top, cap),
        jax.ShapeDtypeStruct((sources, cap, width), BF16),
        [smem] + [vmem] * 4,
        2 * slots * tokens * width,
        3 * slots * width,
    )(at, block, *others)
    rows = lax.all_to_all(
        picked.reshape(16, 4, cap, width), ("x", "b0", "c"), split_axis=0, concat_axis=0, tiled=True
    )
    rows = rows.reshape(4, 4, 4, cap, width).transpose(2, 0, 1, 3, 4).reshape(4, 4, share, width)
    acts = hidden_slots.reshape(4, 4, share, hidden)

    half = hidden // 2
    rides, *u = pl.pallas_call(
        project_kernel,
        out_shape=[array(rider), array(2 * share)]
        + [array(2 * share + rider)] * 3
        + [array(2 * share)] * 4,
        in_specs=[smem] + [vmem] * 3,
        out_specs=[vmem] * 9,
        scratch_shapes=[pltpu.VMEM((4 * share, hidden), BF16)],
        compiler_params=pltpu.CompilerParams(vmem_limit_bytes=VMEM_LIMIT),
        cost_estimate=pl.CostEstimate(
            flops=2 * slots * width * hidden,
            bytes_accessed=2 * slots * (width + hidden),
            transcendentals=0,
        ),
    )(at, rows, w_down[0], acts)
    came = [ahead(u[r], "y", r) for r in (1, 2, 3)]
    came[0], late = lax.optimization_barrier((came[0], u[4:]))
    a, b, slot_gate = call(
        first_kernel,
        [array(2 * share, half)] * 2 + [jax.ShapeDtypeStruct((4, 4 * share), F32)],
        [vmem] * 5,
        8 * share * hidden,
        20 * share * hidden,
    )(u[0], rides, *came)
    a, b = ahead(a, "zh", 1), ahead(b, "zh", -1)
    came = [ahead(late[r], "y", r) for r in (1, 2, 3)]

    slot_gate = slot_gate.reshape(4, 4, share).transpose(1, 0, 2).reshape(sources, cap)
    returned = lax.all_to_all(slot_gate, EXPERT, split_axis=0, concat_axis=0, tiled=True)
    gate_part = call(
        route_kernel, jax.ShapeDtypeStruct((top, tokens), F32), [vmem] * 3, 1 << 20, 1 << 16
    )(ids, gates, returned)

    one, three, own, rides = call(
        second_kernel,
        [array(share + rider, half)] * 2
        + [jax.ShapeDtypeStruct((share, hidden), F32), array(rider, half)],
        [vmem] * 7,
        16 * share * hidden,
        32 * share * hidden,
    )(late[0], gate_part, *came, a, b)
    d_hidden, d_gate = call(
        finish_kernel,
        [array(share), jax.ShapeDtypeStruct((top, tokens), F32)],
        [vmem] * 5,
        4 * share * hidden,
        8 * share * hidden,
    )(own, ahead(one, "zh", 1), ahead(three, "zh", -1), rides, ahead(rides, "zh", 2))
    d_wdown = call(
        weights_kernel,
        array(width),
        [vmem] * 2,
        2 * slots * width * hidden,
        2 * slots * (width + hidden),
    )(rows, acts)
    return d_hidden.reshape(1, 4, cap, hidden), d_gate.T, d_wdown[None]


def solution(mesh):
    fine = Mesh(mesh.devices.reshape(4, 4, 4, 2, 2, 2, 2), ("zh", "y") + EXPERT)
    dp = ("zh", "y")
    return jax.shard_map(
        on_device,
        mesh=fine,
        in_specs=(
            P(EXPERT, dp),
            P(EXPERT, None),
            P(EXPERT, None),
            P(EXPERT, dp, None),
            P(EXPERT, None, None, None),
        ),
        out_specs=(P(EXPERT, dp, None, None), P(EXPERT, None), P(EXPERT, dp, None)),
        check_vma=False,
    )
```
